32 devices in a mesh: shard: 16 (over z, y, x), rep: 2 (over core).
Axes of the slice: x: 2, y: 2, z: 4, core: 2. Of those that a mesh axis runs over, the one named last changes fastest.
Arguments:
- left: bfloat16 [16384, 1024], P(('shard', 'rep')), may hold values from -110 to 110
- catalog: bfloat16 [32768, 1792], P('shard'), may hold values from -16 to 16
- probes: int32 [32, 25], P(('shard', 'rep')), may hold values from -1 to 127, as said below
- perm: int32 [16384], P(('shard', 'rep')), may hold values from 0 to 16383, as said below
Outputs:
- result: bfloat16 [16384, 768], P(('shard', 'rep'))
The draws below stay inside these ranges and needn't reach their ends.
Inputs may be any that keep to these rules, and one draw needn't show every extreme that they name: `probes`: each row lists, for each of the 5 owners nearest to its left block's shard index (offsets -2 to 2, modulo the number of shard indices), between 3 and 5 distinct blocks of that owner; all other entries are -1; entries in random order. In every draw some row lists 5 blocks on each of these owners. `perm`: A permutation; the rows of each left block go to each left block exactly 512 // 32 times.
All inputs are finite; a program needn't handle non-finite values.
Results may differ from the reference program's by a relative error of at most 0.0033.
Values may be sent and summed in bfloat16 or wider, within the bound.
A program may use at most 128 MiB of HBM per device.

```python
import math
import jax
import jax.numpy as jnp
from jax import lax

D = 1024
A = 768
BLK = 256
Q = 512
CB_DEV = 8
REACH = 2
CAP = 5
LEFT_BLOCKS = 32
LEFT_ROWS = 16384
CAT_BLOCKS = 128
CAT_ROWS = 32768


def draw_left(key, part):
    base = jnp.clip(jax.random.normal(key, (LEFT_ROWS, D), jnp.float32), -6.0, 6.0)
    return base.astype(jnp.bfloat16)


def draw_catalog(key, part):
    key_part = jnp.clip(jax.random.normal(jax.random.fold_in(key, 1), (CAT_ROWS, D), jnp.float32), -6.0, 6.0)
    value_part = 2.0 * jnp.clip(jax.random.normal(jax.random.fold_in(key, 2), (CAT_ROWS, A), jnp.float32), -6.0, 6.0)
    return jnp.concatenate([key_part, value_part], axis=1).astype(jnp.bfloat16)


def draw_probes(key, part):
    groups = 2 * REACH + 1
    shard_count = CAT_BLOCKS // CB_DEV
    rep_count = LEFT_BLOCKS // shard_count
    extra = jax.random.randint(jax.random.fold_in(key, 11), (LEFT_BLOCKS,), 1, 2 * groups + 1)
    chosen = jax.random.randint(jax.random.fold_in(key, 12), (), 0, LEFT_BLOCKS)
    extra = jnp.where(jnp.arange(LEFT_BLOCKS) == chosen, 2 * groups, extra)
    ranks = jax.vmap(lambda k: jax.random.permutation(k, groups))(jax.random.split(jax.random.fold_in(key, 13), LEFT_BLOCKS))
    counts = CAP - 2 + extra[:, None] // groups + (ranks < (extra % groups)[:, None]).astype(jnp.int32)
    picks = jax.vmap(lambda k: jax.random.permutation(k, CB_DEV))(jax.random.split(jax.random.fold_in(key, 14), LEFT_BLOCKS * groups))
    picks = picks.reshape(LEFT_BLOCKS, groups, CB_DEV)[:, :, :CAP]
    home = jnp.arange(LEFT_BLOCKS) // rep_count
    owners = (home[:, None] + jnp.arange(groups)[None, :] - REACH) % shard_count
    listed = owners[:, :, None] * CB_DEV + picks
    keep = jnp.arange(CAP)[None, None, :] < counts[:, :, None]
    listed = jnp.where(keep, listed, -1).reshape(LEFT_BLOCKS, groups * CAP)
    shuffle = jax.vmap(lambda k: jax.random.permutation(k, groups * CAP))(jax.random.split(jax.random.fold_in(key, 15), LEFT_BLOCKS))
    return jnp.take_along_axis(listed, shuffle, axis=1).astype(jnp.int32)


def draw_perm(key, part):
    each = Q // LEFT_BLOCKS
    items = jax.vmap(lambda k: jax.random.permutation(k, Q))(jax.random.split(jax.random.fold_in(key, 21), LEFT_BLOCKS))
    landing = jax.vmap(lambda k: jax.random.permutation(k, Q))(jax.random.split(jax.random.fold_in(key, 22), LEFT_BLOCKS))
    target_block = items // each
    within = items % each
    source = jnp.arange(LEFT_BLOCKS)[:, None]
    target_row = landing[target_block, source * each + within]
    return (target_block * Q + target_row).reshape(-1).astype(jnp.int32)


def setup_inputs(seed: int = 0) -> dict:
    arg_keys = jax.random.split(jax.random.key(seed), 5)
    left = draw_left(jax.random.fold_in(arg_keys[4], 71), 0)
    catalog = draw_catalog(jax.random.fold_in(arg_keys[4], 71), 0)
    probes = draw_probes(jax.random.fold_in(arg_keys[4], 71), 0)
    perm = draw_perm(jax.random.fold_in(arg_keys[4], 71), 0)
    return dict(left=left, catalog=catalog, probes=probes, perm=perm)


def slots_for(listed, owner):
    hit = (listed >= 0) & (listed // CB_DEV == owner)
    places = jnp.cumsum(hit.astype(jnp.int32)) - 1
    target = jnp.where(hit, places, CAP).astype(jnp.int32)
    filled = jnp.full((CAP + 1,), -1, jnp.int32).at[target].set(jnp.where(hit, listed % CB_DEV, -1).astype(jnp.int32))
    slots = filled[:CAP]
    return (slots, slots >= 0)

def group_partial(queries_in, blocks, valid):
    key_part = blocks[:, :, :D].astype(jnp.float32)
    value_part = blocks[:, :, D:].astype(jnp.float32)
    scores = jnp.einsum('qd,cbd->qcb', queries_in.astype(jnp.float32), key_part) * (2.5 / math.sqrt(D))
    scores = jnp.where(valid[None, :, None], scores, -jnp.inf)
    group_max = lax.optimization_barrier(jnp.max(scores, axis=(1, 2)))
    expos = jnp.exp(scores - group_max[:, None, None])
    group_total = lax.optimization_barrier(jnp.sum(expos, axis=(1, 2)))
    weights = lax.optimization_barrier(expos.astype(jnp.bfloat16))
    group_acc = jnp.einsum('qcb,cba->qa', weights.astype(jnp.float32), value_part)
    return (group_max, group_total, group_acc)

def combine_groups(parts):
    peak = parts[0][0]
    for part in parts[1:]:
        peak = jnp.maximum(peak, part[0])
    numer = jnp.zeros_like(parts[0][2])
    denom = jnp.zeros_like(parts[0][1])
    for part in parts:
        factor = jnp.exp(part[0] - peak)
        numer = numer + factor[:, None] * part[2]
        denom = denom + factor * part[1]
    return (numer / denom[:, None]).astype(jnp.bfloat16)

def reference(left, catalog, probes, perm):
    table = catalog.reshape(CAT_BLOCKS, BLK, D + A)
    shard_count = CAT_BLOCKS // CB_DEV
    rep_count = LEFT_BLOCKS // shard_count

    def one_block(index):
        queries_in = lax.dynamic_slice_in_dim(left, (index * Q).astype(jnp.int32), Q, 0)
        listed = probes[index]
        home = index // rep_count
        parts = []
        for offset in range(-REACH, REACH + 1):
            owner = (home + offset) % shard_count
            slots, valid = slots_for(listed, owner)
            blocks = table[(owner * CB_DEV + jnp.maximum(slots, 0)).astype(jnp.int32)]
            parts.append(group_partial(queries_in, blocks, valid))
        return combine_groups(parts)
    joined = lax.map(one_block, jnp.arange(LEFT_BLOCKS, dtype=jnp.int32)).reshape(LEFT_ROWS, A)
    return jnp.zeros((LEFT_ROWS, A), jnp.bfloat16).at[perm].set(joined)
```

```python
import math

import jax
import jax.numpy as jnp
from jax import lax
from jax.experimental import pallas as pl
from jax.experimental.pallas import tpu as pltpu
from jax.sharding import PartitionSpec as P

D = 1024
A = 768
BLK = 256
CB_DEV = 8
REACH = 2
CAP = 5
SCALE = 2.5 / math.sqrt(D)
NT = (((1,), (1,)), ((), ()))


def shifted(block, axis, distance):
    devices = range(lax.axis_size(axis))
    route = [((i - distance) % len(devices), i) for i in devices]
    return lax.ppermute(block, axis, route)


def slots_for(listed, owner):
    hit = (listed >= 0) & (listed // CB_DEV == owner)
    places = jnp.cumsum(hit.astype(jnp.int32)) - 1
    chosen = hit[None, :] & (places[None, :] == jnp.arange(CAP)[:, None])
    return jnp.max(jnp.where(chosen, listed[None, :] % CB_DEV, -1), axis=1)


def group_kernel(slots_ref, q_ref, *refs):
    blocks, (acc_ref, stat_ref) = refs[:CAP], refs[CAP:]
    q = q_ref[...]
    scores = []
    for j in range(CAP):
        s = lax.dot_general(q, blocks[j][:, :D], NT, preferred_element_type=jnp.float32) * SCALE
        scores.append(jnp.where(slots_ref[j] >= 0, s, -jnp.inf))
    peak = scores[0]
    for s in scores[1:]:
        peak = jnp.maximum(peak, s)
    peak = jnp.max(peak, axis=1, keepdims=True)
    total = jnp.zeros_like(peak)
    acc = None
    for j in range(CAP):
        e = jnp.exp(scores[j] - peak)
        total = total + jnp.sum(e, axis=1, keepdims=True)
        part = jnp.dot(e.astype(jnp.bfloat16), blocks[j][:, D:], preferred_element_type=jnp.float32)
        acc = part if acc is None else acc + part
    acc_ref[...] = acc.astype(acc_ref.dtype)
    lane = lax.broadcasted_iota(jnp.int32, (q.shape[0], 128), 1)
    stat = jnp.where(lane == 0, peak, total)
    stat_ref[...] = stat.T[:8, :]


def group_partial(q, catalog, slots, dtype):
    rows = q.shape[0]
    chunk = 256
    return pl.pallas_call(
        group_kernel,
        grid_spec=pltpu.PrefetchScalarGridSpec(
            num_scalar_prefetch=1,
            grid=(rows // chunk,),
            in_specs=[pl.BlockSpec((chunk, D), lambda i, s: (i, 0))]
            + [
                pl.BlockSpec((BLK, D + A), lambda i, s, j=j: (jnp.maximum(s[j], 0), 0))
                for j in range(CAP)
            ],
            out_specs=[
                pl.BlockSpec((chunk, A), lambda i, s: (i, 0)),
                pl.BlockSpec((8, chunk), lambda i, s: (0, i)),
            ],
        ),
        out_shape=[
            jax.ShapeDtypeStruct((rows, A), dtype),
            jax.ShapeDtypeStruct((8, rows), jnp.float32),
        ],
        compiler_params=pltpu.CompilerParams(vmem_limit_bytes=40 * 1024 * 1024),
        cost_estimate=pl.CostEstimate(
            flops=2 * rows * CAP * BLK * (D + A),
            bytes_accessed=CAP * BLK * (D + A) * 2 + rows * (D + 2 * A) * 2,
            transcendentals=rows * CAP * BLK,
        ),
    )(slots, q, *([catalog] * CAP))


def body(left, catalog, probes, perm):
    shard_count = lax.axis_size("shard")
    rep_count = lax.axis_size("rep")
    own = lax.axis_index("shard")
    block_rows = left.shape[0]
    devices = shard_count * rep_count
    rows_each = block_rows // devices
    offsets = (2, -2, 1, -1)
    moved = {k: shifted(left, "shard", k) for k in offsets}
    lists = {k: shifted(probes, "shard", k) for k in offsets}

    target_device = perm // block_rows
    target_row = perm % block_rows
    index = jnp.arange(block_rows)
    earlier = (target_device[:, None] == target_device[None, :]) & (index[None, :] < index[:, None])
    place = target_device * rows_each + jnp.sum(earlier.astype(jnp.int32), axis=1)
    order = place[None, :] == index[:, None]
    positions = jnp.sum(jnp.where(order, target_row[None, :], 0), axis=1).astype(jnp.int32)
    landing = lax.all_to_all(
        positions.reshape(devices, rows_each), ("shard", "rep"), 0, 0, tiled=True
    ).reshape(-1)

    parts = [group_partial(left, catalog, slots_for(probes[0], own), jnp.float32)]
    for k in offsets:
        acc, stat = group_partial(
            moved[k], catalog, slots_for(lists[k][0], own), jnp.bfloat16
        )
        parts.append((shifted(acc, "shard", -k), shifted(stat[:2], "shard", -k)))
    peak = parts[0][1][0]
    for part in parts[1:]:
        peak = jnp.maximum(peak, part[1][0])
    numer = jnp.zeros((block_rows, A), jnp.float32)
    denom = jnp.zeros((block_rows,), jnp.float32)
    for acc, stat in parts:
        factor = jnp.exp(stat[0] - peak)
        numer = numer + factor[:, None] * acc.astype(jnp.float32)
        denom = denom + factor * stat[1]
    joined = (numer / denom[:, None]).astype(jnp.bfloat16)

    outgoing = jnp.dot(
        order.astype(jnp.bfloat16), joined, preferred_element_type=jnp.float32
    ).astype(jnp.bfloat16)
    arrived = lax.all_to_all(
        outgoing.reshape(devices, rows_each, A), ("shard", "rep"), 0, 0, tiled=True
    ).reshape(block_rows, A)
    spread = (landing[None, :] == index[:, None]).astype(jnp.bfloat16)
    return jnp.dot(spread, arrived, preferred_element_type=jnp.float32).astype(jnp.bfloat16)


def solution(mesh):
    placed = (
        P(("shard", "rep"), None),
        P("shard", None),
        P(("shard", "rep"), None),
        P(("shard", "rep")),
    )
    return jax.shard_map(
        body, mesh=mesh, in_specs=placed, out_specs=P(("shard", "rep"), None), check_vma=False
    )
```

```python
import functools
import math

import jax
import jax.numpy as jnp
from jax import lax
from jax.experimental import pallas as pl
from jax.experimental.pallas import tpu as pltpu
from jax.sharding import PartitionSpec as P

D = 1024
A = 768
BLK = 256
CB_DEV = 8
REACH = 2
CAP = 5
SCALE = 2.5 / math.sqrt(D)
NT = (((1,), (1,)), ((), ()))


def shifted(block, axis, distance):
    devices = range(lax.axis_size(axis))
    route = [((i - distance) % len(devices), i) for i in devices]
    return lax.ppermute(block, axis, route)


def slots_for(listed, owner):
    hit = (listed >= 0) & (listed // CB_DEV == owner)
    places = jnp.cumsum(hit.astype(jnp.int32)) - 1
    chosen = hit[None, :] & (places[None, :] == jnp.arange(CAP)[:, None])
    return jnp.max(jnp.where(chosen, listed[None, :] % CB_DEV, -1), axis=1)


def group_kernel(slots_ref, q_ref, *refs):
    blocks, (acc_ref, stat_ref) = refs[:CAP], refs[CAP:]
    q = q_ref[...]
    scores = []
    for j in range(CAP):
        s = lax.dot_general(q, blocks[j][:, :D], NT, preferred_element_type=jnp.float32) * SCALE
        scores.append(jnp.where(slots_ref[j] >= 0, s, -jnp.inf))
    peak = scores[0]
    for s in scores[1:]:
        peak = jnp.maximum(peak, s)
    peak = jnp.max(peak, axis=1, keepdims=True)
    total = jnp.zeros_like(peak)
    acc = None
    for j in range(CAP):
        e = jnp.exp(scores[j] - peak)
        total = total + jnp.sum(e, axis=1, keepdims=True)
        part = jnp.dot(e.astype(jnp.bfloat16), blocks[j][:, D:], preferred_element_type=jnp.float32)
        acc = part if acc is None else acc + part
    acc_ref[...] = acc.astype(acc_ref.dtype)
    lane = lax.broadcasted_iota(jnp.int32, (q.shape[0], 128), 1)
    stat = jnp.where(lane == 0, peak, total)
    stat_ref[...] = stat.T[:8, :]


def group_partial(q, catalog, slots, dtype):
    rows = q.shape[0]
    chunk = 256
    return pl.pallas_call(
        group_kernel,
        grid_spec=pltpu.PrefetchScalarGridSpec(
            num_scalar_prefetch=1,
            grid=(rows // chunk,),
            in_specs=[pl.BlockSpec((chunk, D), lambda i, s: (i, 0))]
            + [
                pl.BlockSpec((BLK, D + A), lambda i, s, j=j: (jnp.maximum(s[j], 0), 0))
                for j in range(CAP)
            ],
            out_specs=[
                pl.BlockSpec((chunk, A), lambda i, s: (i, 0)),
                pl.BlockSpec((8, chunk), lambda i, s: (0, i)),
            ],
        ),
        out_shape=[
            jax.ShapeDtypeStruct((rows, A), dtype),
            jax.ShapeDtypeStruct((8, rows), jnp.float32),
        ],
        compiler_params=pltpu.CompilerParams(vmem_limit_bytes=40 * 1024 * 1024),
        cost_estimate=pl.CostEstimate(
            flops=2 * rows * CAP * BLK * (D + A),
            bytes_accessed=CAP * BLK * (D + A) * 2 + rows * (D + 2 * A) * 2,
            transcendentals=rows * CAP * BLK,
        ),
    )(slots, q, *([catalog] * CAP))


def plain_body(left, catalog, probes, perm):
    shard_count = lax.axis_size("shard")
    rep_count = lax.axis_size("rep")
    own = lax.axis_index("shard")
    block_rows = left.shape[0]
    devices = shard_count * rep_count
    rows_each = block_rows // devices
    offsets = (2, -2, 1, -1)
    moved = {k: shifted(left, "shard", k) for k in offsets}
    lists = {k: shifted(probes, "shard", k) for k in offsets}

    target_device = perm // block_rows
    target_row = perm % block_rows
    index = jnp.arange(block_rows)
    earlier = (target_device[:, None] == target_device[None, :]) & (index[None, :] < index[:, None])
    place = target_device * rows_each + jnp.sum(earlier.astype(jnp.int32), axis=1)
    order = place[None, :] == index[:, None]
    positions = jnp.sum(jnp.where(order, target_row[None, :], 0), axis=1).astype(jnp.int32)
    landing = lax.all_to_all(
        positions.reshape(devices, rows_each), ("shard", "rep"), 0, 0, tiled=True
    ).reshape(-1)

    parts = [group_partial(left, catalog, slots_for(probes[0], own), jnp.float32)]
    for k in offsets:
        acc, stat = group_partial(
            moved[k], catalog, slots_for(lists[k][0], own), jnp.bfloat16
        )
        parts.append((shifted(acc, "shard", -k), shifted(stat[:2], "shard", -k)))
    peak = parts[0][1][0]
    for part in parts[1:]:
        peak = jnp.maximum(peak, part[1][0])
    numer = jnp.zeros((block_rows, A), jnp.float32)
    denom = jnp.zeros((block_rows,), jnp.float32)
    for acc, stat in parts:
        factor = jnp.exp(stat[0] - peak)
        numer = numer + factor[:, None] * acc.astype(jnp.float32)
        denom = denom + factor * stat[1]
    joined = (numer / denom[:, None]).astype(jnp.bfloat16)

    outgoing = jnp.dot(
        order.astype(jnp.bfloat16), joined, preferred_element_type=jnp.float32
    ).astype(jnp.bfloat16)
    arrived = lax.all_to_all(
        outgoing.reshape(devices, rows_each, A), ("shard", "rep"), 0, 0, tiled=True
    ).reshape(block_rows, A)
    spread = (landing[None, :] == index[:, None]).astype(jnp.bfloat16)
    return jnp.dot(spread, arrived, preferred_element_type=jnp.float32).astype(jnp.bfloat16)


MESH = pl.DeviceIdType.MESH
ARRIVALS = 4
CHUNKS = 2


def partner_x(s):
    return s + 1 - 2 * (s % 2)


def partner_y(s):
    return s + 2 - 4 * ((s // 2) % 2)


def partner_z(s, n):
    return (s + 4 - 8 * ((s // 2) % 2) + n) % n


def source_z(s, n):
    return (s - 4 + 8 * ((s // 2) % 2) + n) % n


def is_early(s):
    return (s % 4) * (3 - s % 4) == 0


def attend(q, cat, slot_of):
    slots = [slot_of(j) for j in range(CAP)]
    picks = [jnp.maximum(slot, 0) for slot in slots]
    scores = []
    for j in range(CAP):
        keys = cat[picks[j], :, :D]
        s = lax.dot_general(q, keys, NT, preferred_element_type=jnp.float32) * SCALE
        scores.append(jnp.where(slots[j] >= 0, s, -jnp.inf))
    peak = scores[0]
    for s in scores[1:]:
        peak = jnp.maximum(peak, s)
    peak = jnp.max(peak, axis=1, keepdims=True)
    total = jnp.zeros_like(peak)
    acc = None
    for j in range(CAP):
        e = jnp.exp(scores[j] - peak)
        total = total + jnp.sum(e, axis=1, keepdims=True)
        values = cat[picks[j], :, D:]
        part = jnp.dot(e.astype(jnp.bfloat16), values, preferred_element_type=jnp.float32)
        acc = part if acc is None else acc + part
    lane = lax.broadcasted_iota(jnp.int32, (q.shape[0], 128), 1)
    return acc, jnp.where(lane == 0, peak, total)


def fused_kernel(
    n, reps, left, cat_hbm, slots, place, pout, out,
    cat, arr, slotv, slots_sm, accs, stats, acc_in, stat_in, own_acc, own_stat,
    joined, gout, gin, pin,
    cat_sem, slot_local, slot_send, slot_recv, f_send, f_recv,
    r_send, r_recv, s_send, s_recv, p_send, p_recv, p_local, g_send, g_recv, g_local,
):
    count = n * reps
    rows = left.shape[0]
    size = rows // CHUNKS
    each = rows // count
    s = lax.axis_index("shard")
    rep = lax.axis_index("rep")
    me = s * reps + rep
    early = is_early(s)
    px, py, pz = partner_x(s), partner_y(s), partner_z(s, n)
    pyz = partner_z(py, n)
    far = jnp.where(early, partner_x(pyz), partner_x(py))
    dests = [px, py, pyz, far]
    zs = source_z(s, n)
    xz = source_z(px, n)
    origins = [px, py, partner_y(zs), jnp.where(is_early(px), partner_y(px), partner_y(xz))]

    def to(shard):
        return {"shard": shard, "rep": rep}

    def device(d):
        return {"shard": d // reps, "rep": d % reps}

    def remote(src, dst, send, recv, target):
        return pltpu.make_async_remote_copy(
            src_ref=src, dst_ref=dst, send_sem=send, recv_sem=recv,
            device_id=target, device_id_type=MESH,
        )

    def chunk(c):
        return pl.ds(c * size, size)

    cat_copy = pltpu.make_async_copy(cat_hbm, cat, cat_sem)
    cat_copy.start()
    own_slots = pltpu.make_async_copy(slots, slots_sm.at[0], slot_local.at[0])
    own_slots.start()

    barrier = pltpu.get_barrier_semaphore()

    @pl.loop(1, count)
    def _(t):
        pl.semaphore_signal(
            barrier, inc=1, device_id=device((me + t) % count), device_id_type=MESH
        )

    pl.semaphore_wait(barrier, count - 1)

    slot_copies = [
        remote(slots, slotv.at[a], slot_send.at[a], slot_recv.at[a], to(dests[a]))
        for a in range(ARRIVALS)
    ]
    for copy in slot_copies:
        copy.start()

    def hop(src, a, c, target):
        return remote(src, arr.at[a, chunk(c)], f_send.at[a, c], f_recv.at[a, c], to(target))

    def hop_x(c):
        return hop(left.at[chunk(c)], 0, c, px)

    def hop_y(c):
        return hop(left.at[chunk(c)], 1, c, py)

    def hop_z(c):
        return hop(arr.at[1, chunk(c)], 2, c, pz)

    def hop_far(c, a):
        return hop(arr.at[a, chunk(c)], 3, c, px)

    for c in range(CHUNKS):
        hop_y(c).start()
        hop_x(c).start()

    pos_local = pltpu.make_async_copy(pout.at[me], pin.at[me], p_local)
    pos_local.start()

    @pl.loop(1, count)
    def _(t):
        d = (me + t) % count
        remote(pout.at[d], pin.at[me], p_send, p_recv, device(d)).start()

    cat_copy.wait()
    own_slots.wait()
    for c in range(CHUNKS):
        acc, stat = attend(left[chunk(c)], cat, lambda j: slots_sm[0, 0, j])
        own_acc[chunk(c)] = acc
        own_stat[chunk(c)] = stat

    for a in range(ARRIVALS):
        slot_copies[a].wait_recv()
        local = pltpu.make_async_copy(slotv.at[a], slots_sm.at[1 + a], slot_local.at[1 + a])
        local.start()
        local.wait()

    def back(a, c):
        return (
            remote(accs.at[a, chunk(c)], acc_in.at[a, chunk(c)], r_send.at[a, c],
                   r_recv.at[a, c], to(origins[a])),
            remote(stats.at[a, c], stat_in.at[a, c], s_send.at[a, c],
                   s_recv.at[a, c], to(origins[a])),
        )

    def serve(a, c):
        acc, stat = attend(arr[a, chunk(c)], cat, lambda j: slots_sm[1 + a, 1 + a, j])
        accs[a, chunk(c)] = acc.astype(jnp.bfloat16)
        stats[a, c] = stat.T[:8, :]
        for copy in back(a, c):
            copy.start()

    def take_y(c):
        hop_y(c).wait_recv()
        hop_z(c).start()

        @pl.when(early)
        def _():
            hop_far(c, 1).start()

    def take_z(c):
        hop_z(c).wait_recv()

        @pl.when(jnp.logical_not(early))
        def _():
            hop_far(c, 2).start()

    take_y(0)
    serve(1, 0)
    hop_x(0).wait_recv()
    serve(0, 0)
    take_y(1)
    take_z(0)
    serve(1, 1)
    serve(2, 0)
    hop_x(1).wait_recv()
    serve(0, 1)
    take_z(1)
    hop_far(0, 1).wait_recv()
    serve(3, 0)
    serve(2, 1)
    hop_far(1, 1).wait_recv()
    serve(3, 1)

    for c in range(CHUNKS):
        for a in range(ARRIVALS):
            for copy in back(a, c):
                copy.wait_recv()
        columns = [own_stat[chunk(c)]]
        for a in range(ARRIVALS):
            columns.append(jnp.concatenate([stat_in[a, c]] * 16, axis=0).T)
        peak = columns[0][:, 0:1]
        for column in columns[1:]:
            peak = jnp.maximum(peak, column[:, 0:1])
        factor = jnp.exp(columns[0][:, 0:1] - peak)
        numer = factor * own_acc[chunk(c)]
        denom = factor * columns[0][:, 1:2]
        for a in range(ARRIVALS):
            factor = jnp.exp(columns[1 + a][:, 0:1] - peak)
            numer = numer + factor * acc_in[a, chunk(c)].astype(jnp.float32)
            denom = denom + factor * columns[1 + a][:, 1:2]
        joined[chunk(c)] = (numer / denom).astype(jnp.bfloat16)

    index = lax.broadcasted_iota(jnp.int32, (rows, rows), 0)
    order = jnp.where(index == place[0:1, :], 1.0, 0.0).astype(jnp.bfloat16)
    gout[...] = jnp.dot(order, joined[...], preferred_element_type=jnp.float32).astype(jnp.bfloat16)

    def lot(d):
        return pl.ds(pl.multiple_of(d * each, each), each)

    row_local = pltpu.make_async_copy(gout.at[lot(me)], gin.at[lot(me)], g_local)
    row_local.start()

    @pl.loop(1, count)
    def _(t):
        d = (me + t) % count
        remote(gout.at[lot(d)], gin.at[lot(me)], g_send, g_recv, device(d)).start()

    for c in range(CHUNKS):
        for a in range(ARRIVALS):
            for copy in back(a, c):
                copy.wait_send()
        hop_x(c).wait_send()
        hop_y(c).wait_send()
        hop_z(c).wait_send()
        hop_far(c, 1).wait_send()
    for copy in slot_copies:
        copy.wait_send()
    other = device((me + 1) % count)
    pos = remote(pout.at[pl.ds(0, count - 1)], pin.at[pl.ds(0, count - 1)], p_send, p_recv, other)
    pos.wait_send()
    pos.wait_recv()
    pos_local.wait()
    per = 128 // each
    groups = rows // 128
    landing = jnp.sum(pin[...].reshape(groups, per, 8, 128), axis=1)
    iota = lax.broadcasted_iota(jnp.int32, (rows, 128), 0)
    spread = jnp.concatenate(
        [jnp.where(iota == landing[g, 0:1, :], 1.0, 0.0) for g in range(groups)], axis=1
    ).astype(jnp.bfloat16)

    most = pl.ds(0, (count - 1) * each)
    sent = remote(gout.at[most], gin.at[most], g_send, g_recv, other)
    sent.wait_send()
    sent.wait_recv()
    row_local.wait()
    out[...] = jnp.dot(spread, gin[...], preferred_element_type=jnp.float32).astype(jnp.bfloat16)


def fused_body(left, catalog, probes, perm):
    n = lax.axis_size("shard")
    reps = lax.axis_size("rep")
    s = lax.axis_index("shard")
    me = s * reps + lax.axis_index("rep")
    rows = left.shape[0]
    count = n * reps
    each = rows // count

    py = partner_y(s)
    pyz = partner_z(py, n)
    far = jnp.where(is_early(s), partner_x(pyz), partner_x(py))
    owners = jnp.stack([s, partner_x(s), py, pyz, far])
    listed = probes[0]
    hit = (listed[None, :] >= 0) & (listed[None, :] // CB_DEV == owners[:, None])
    places = jnp.cumsum(hit.astype(jnp.int32), axis=1) - 1
    chosen = hit[:, None, :] & (places[:, None, :] == jnp.arange(CAP)[None, :, None])
    slots = jnp.max(jnp.where(chosen, listed[None, None, :] % CB_DEV, -1), axis=2)
    slots = jnp.pad(slots.astype(jnp.int32), ((0, 3), (0, 128 - CAP)))

    target_device = perm // rows
    target_row = perm % rows
    index = jnp.arange(rows)
    earlier = (target_device[:, None] == target_device[None, :]) & (index[None, :] < index[:, None])
    place = target_device * each + jnp.sum(earlier.astype(jnp.int32), axis=1)
    lane = jnp.arange(128)
    first = (me * each) % 128
    local = lane - first
    wanted = jnp.where((local >= 0) & (local < each), local, -rows)[None, :] + (
        jnp.arange(count) * each
    )[:, None]
    pout = jnp.sum(
        jnp.where(wanted[:, :, None] == place[None, None, :], target_row[None, None, :], 0), axis=2
    ).astype(jnp.int32)
    pout = jnp.broadcast_to(pout[:, None, :], (count, 8, 128))
    place = jnp.broadcast_to(place.astype(jnp.int32)[None, :], (8, rows))

    bf16, f32, i32 = jnp.bfloat16, jnp.float32, jnp.int32
    size = rows // CHUNKS
    dma = pltpu.SemaphoreType.DMA
    vmem = pl.BlockSpec(memory_space=pltpu.VMEM)
    return pl.pallas_call(
        functools.partial(fused_kernel, n, reps),
        out_shape=jax.ShapeDtypeStruct((rows, A), bf16),
        in_specs=[vmem, pl.BlockSpec(memory_space=pl.ANY), vmem, vmem, vmem],
        out_specs=vmem,
        scratch_shapes=[
            pltpu.VMEM((CB_DEV, BLK, D + A), bf16),
            pltpu.VMEM((ARRIVALS, rows, D), bf16),
            pltpu.VMEM((ARRIVALS, 8, 128), i32),
            pltpu.SMEM((ARRIVALS + 1, 8, 128), i32),
            pltpu.VMEM((ARRIVALS, rows, A), bf16),
            pltpu.VMEM((ARRIVALS, CHUNKS, 8, size), f32),
            pltpu.VMEM((ARRIVALS, rows, A), bf16),
            pltpu.VMEM((ARRIVALS, CHUNKS, 8, size), f32),
            pltpu.VMEM((rows, A), f32),
            pltpu.VMEM((rows, 128), f32),
            pltpu.VMEM((rows, A), bf16),
            pltpu.VMEM((rows, A), bf16),
            pltpu.VMEM((rows, A), bf16),
            pltpu.VMEM((count, 8, 128), i32),
            dma, dma((ARRIVALS + 1,)), dma((ARRIVALS,)), dma((ARRIVALS,)),
            dma((ARRIVALS, CHUNKS)), dma((ARRIVALS, CHUNKS)),
            dma((ARRIVALS, CHUNKS)), dma((ARRIVALS, CHUNKS)),
            dma((ARRIVALS, CHUNKS)), dma((ARRIVALS, CHUNKS)),
            dma, dma, dma, dma, dma, dma,
        ],
        compiler_params=pltpu.CompilerParams(
            collective_id=0, has_side_effects=True, vmem_limit_bytes=48 * 1024 * 1024
        ),
        cost_estimate=pl.CostEstimate(
            flops=10 * rows * CAP * BLK * (D + A),
            bytes_accessed=catalog.size * 2 + rows * (D + A) * 2,
            transcendentals=5 * rows * CAP * BLK,
        ),
    )(left, catalog.reshape(CB_DEV, BLK, D + A), slots, place, pout)


def body(left, catalog, probes, perm):
    n = lax.axis_size("shard")
    each = left.shape[0] // (n * lax.axis_size("rep"))
    if each % 16 == 0 and 128 % each == 0 and n % 4 == 0 and n >= 16:
        return fused_body(left, catalog, probes, perm)
    return plain_body(left, catalog, probes, perm)


def solution(mesh):
    placed = (
        P(("shard", "rep"), None),
        P("shard", None),
        P(("shard", "rep"), None),
        P(("shard", "rep")),
    )
    return jax.shard_map(
        body, mesh=mesh, in_specs=placed, out_specs=P(("shard", "rep"), None), check_vma=False
    )
```

```python
import functools
import math

import jax
import jax.numpy as jnp
from jax import lax
from jax.experimental import pallas as pl
from jax.experimental.pallas import tpu as pltpu
from jax.sharding import PartitionSpec as P

D = 1024
A = 768
BLK = 256
CB_DEV = 8
REACH = 2
CAP = 5
SCALE = 2.5 / math.sqrt(D)
NT = (((1,), (1,)), ((), ()))


def shifted(block, axis, distance):
    devices = range(lax.axis_size(axis))
    route = [((i - distance) % len(devices), i) for i in devices]
    return lax.ppermute(block, axis, route)


def slots_for(listed, owner):
    hit = (listed >= 0) & (listed // CB_DEV == owner)
    places = jnp.cumsum(hit.astype(jnp.int32)) - 1
    chosen = hit[None, :] & (places[None, :] == jnp.arange(CAP)[:, None])
    return jnp.max(jnp.where(chosen, listed[None, :] % CB_DEV, -1), axis=1)


def group_kernel(slots_ref, q_ref, *refs):
    blocks, (acc_ref, stat_ref) = refs[:CAP], refs[CAP:]
    q = q_ref[...]
    scores = []
    for j in range(CAP):
        s = lax.dot_general(q, blocks[j][:, :D], NT, preferred_element_type=jnp.float32) * SCALE
        scores.append(jnp.where(slots_ref[j] >= 0, s, -jnp.inf))
    peak = scores[0]
    for s in scores[1:]:
        peak = jnp.maximum(peak, s)
    peak = jnp.max(peak, axis=1, keepdims=True)
    total = jnp.zeros_like(peak)
    acc = None
    for j in range(CAP):
        e = jnp.exp(scores[j] - peak)
        total = total + jnp.sum(e, axis=1, keepdims=True)
        part = jnp.dot(e.astype(jnp.bfloat16), blocks[j][:, D:], preferred_element_type=jnp.float32)
        acc = part if acc is None else acc + part
    acc_ref[...] = acc.astype(acc_ref.dtype)
    lane = lax.broadcasted_iota(jnp.int32, (q.shape[0], 128), 1)
    stat = jnp.where(lane == 0, peak, total)
    stat_ref[...] = stat.T[:8, :]


def group_partial(q, catalog, slots, dtype):
    rows = q.shape[0]
    chunk = 256
    return pl.pallas_call(
        group_kernel,
        grid_spec=pltpu.PrefetchScalarGridSpec(
            num_scalar_prefetch=1,
            grid=(rows // chunk,),
            in_specs=[pl.BlockSpec((chunk, D), lambda i, s: (i, 0))]
            + [
                pl.BlockSpec((BLK, D + A), lambda i, s, j=j: (jnp.maximum(s[j], 0), 0))
                for j in range(CAP)
            ],
            out_specs=[
                pl.BlockSpec((chunk, A), lambda i, s: (i, 0)),
                pl.BlockSpec((8, chunk), lambda i, s: (0, i)),
            ],
        ),
        out_shape=[
            jax.ShapeDtypeStruct((rows, A), dtype),
            jax.ShapeDtypeStruct((8, rows), jnp.float32),
        ],
        compiler_params=pltpu.CompilerParams(vmem_limit_bytes=40 * 1024 * 1024),
        cost_estimate=pl.CostEstimate(
            flops=2 * rows * CAP * BLK * (D + A),
            bytes_accessed=CAP * BLK * (D + A) * 2 + rows * (D + 2 * A) * 2,
            transcendentals=rows * CAP * BLK,
        ),
    )(slots, q, *([catalog] * CAP))


def plain_body(left, catalog, probes, perm):
    shard_count = lax.axis_size("shard")
    rep_count = lax.axis_size("rep")
    own = lax.axis_index("shard")
    block_rows = left.shape[0]
    devices = shard_count * rep_count
    rows_each = block_rows // devices
    offsets = (2, -2, 1, -1)
    moved = {k: shifted(left, "shard", k) for k in offsets}
    lists = {k: shifted(probes, "shard", k) for k in offsets}

    target_device = perm // block_rows
    target_row = perm % block_rows
    index = jnp.arange(block_rows)
    earlier = (target_device[:, None] == target_device[None, :]) & (index[None, :] < index[:, None])
    place = target_device * rows_each + jnp.sum(earlier.astype(jnp.int32), axis=1)
    order = place[None, :] == index[:, None]
    positions = jnp.sum(jnp.where(order, target_row[None, :], 0), axis=1).astype(jnp.int32)
    landing = lax.all_to_all(
        positions.reshape(devices, rows_each), ("shard", "rep"), 0, 0, tiled=True
    ).reshape(-1)

    parts = [group_partial(left, catalog, slots_for(probes[0], own), jnp.float32)]
    for k in offsets:
        acc, stat = group_partial(
            moved[k], catalog, slots_for(lists[k][0], own), jnp.bfloat16
        )
        parts.append((shifted(acc, "shard", -k), shifted(stat[:2], "shard", -k)))
    peak = parts[0][1][0]
    for part in parts[1:]:
        peak = jnp.maximum(peak, part[1][0])
    numer = jnp.zeros((block_rows, A), jnp.float32)
    denom = jnp.zeros((block_rows,), jnp.float32)
    for acc, stat in parts:
        factor = jnp.exp(stat[0] - peak)
        numer = numer + factor[:, None] * acc.astype(jnp.float32)
        denom = denom + factor * stat[1]
    joined = (numer / denom[:, None]).astype(jnp.bfloat16)

    outgoing = jnp.dot(
        order.astype(jnp.bfloat16), joined, preferred_element_type=jnp.float32
    ).astype(jnp.bfloat16)
    arrived = lax.all_to_all(
        outgoing.reshape(devices, rows_each, A), ("shard", "rep"), 0, 0, tiled=True
    ).reshape(block_rows, A)
    spread = (landing[None, :] == index[:, None]).astype(jnp.bfloat16)
    return jnp.dot(spread, arrived, preferred_element_type=jnp.float32).astype(jnp.bfloat16)


MESH = pl.DeviceIdType.MESH
ARRIVALS = 4
CHUNKS = 2


def partner_x(s):
    return s + 1 - 2 * (s % 2)


def partner_y(s):
    return s + 2 - 4 * ((s // 2) % 2)


def partner_z(s, n):
    return (s + 4 - 8 * ((s // 2) % 2) + n) % n


def source_z(s, n):
    return (s - 4 + 8 * ((s // 2) % 2) + n) % n


def is_early(s):
    return (s % 4) * (3 - s % 4) == 0


def attend(q, cat, slot_of):
    slots = [slot_of(j) for j in range(CAP)]
    picks = [jnp.maximum(slot, 0) for slot in slots]
    scores = []
    for j in range(CAP):
        keys = cat[picks[j], :, :D]
        s = lax.dot_general(q, keys, NT, preferred_element_type=jnp.float32) * SCALE
        scores.append(jnp.where(slots[j] >= 0, s, -jnp.inf))
    peak = scores[0]
    for s in scores[1:]:
        peak = jnp.maximum(peak, s)
    peak = jnp.max(peak, axis=1, keepdims=True)
    total = jnp.zeros_like(peak)
    acc = None
    for j in range(CAP):
        e = jnp.exp(scores[j] - peak)
        total = total + jnp.sum(e, axis=1, keepdims=True)
        values = cat[picks[j], :, D:]
        part = jnp.dot(e.astype(jnp.bfloat16), values, preferred_element_type=jnp.float32)
        acc = part if acc is None else acc + part
    lane = lax.broadcasted_iota(jnp.int32, (q.shape[0], 128), 1)
    return acc, jnp.where(lane == 0, peak, total)


def fused_kernel(
    n, reps, left_hbm, cat_hbm, slots, perm, out,
    raw, left, pout, cat, arr, slotv, slots_sm, accs, stats, acc_in, stat_in, own_acc, own_stat,
    joined, gin, pin,
    left_sem, cat_sem, slot_local, slot_send, slot_recv, f_send, f_recv,
    r_send, r_recv, s_send, s_recv, p_send, p_recv, p_local, g_send, g_recv, g_local,
):
    count = n * reps
    rows = left.shape[0]
    size = rows // CHUNKS
    each = rows // count
    s = lax.axis_index("shard")
    rep = lax.axis_index("rep")
    me = s * reps + rep
    early = is_early(s)
    px, py, pz = partner_x(s), partner_y(s), partner_z(s, n)
    pyz = partner_z(py, n)
    far = jnp.where(early, partner_x(pyz), partner_x(py))
    dests = [px, py, pyz, far]
    zs = source_z(s, n)
    xz = source_z(px, n)
    origins = [px, py, partner_y(zs), jnp.where(is_early(px), partner_y(px), partner_y(xz))]

    def to(shard):
        return {"shard": shard, "rep": rep}

    def device(d):
        return {"shard": d // reps, "rep": d % reps}

    def remote(src, dst, send, recv, target):
        return pltpu.make_async_remote_copy(
            src_ref=src, dst_ref=dst, send_sem=send, recv_sem=recv,
            device_id=target, device_id_type=MESH,
        )

    def chunk(c):
        return pl.ds(c * size, size)

    left_copy = pltpu.make_async_copy(left_hbm, raw, left_sem)
    left_copy.start()
    cat_copy = pltpu.make_async_copy(cat_hbm, cat, cat_sem)
    cat_copy.start()
    own_slots = pltpu.make_async_copy(slots, slots_sm.at[0], slot_local.at[0])
    own_slots.start()

    barrier = pltpu.get_barrier_semaphore()

    @pl.loop(1, count)
    def _(t):
        pl.semaphore_signal(
            barrier, inc=1, device_id=device((me + t) % count), device_id_type=MESH
        )

    bf16, f32, i32 = jnp.bfloat16, jnp.float32, jnp.int32
    iota = lax.broadcasted_iota
    target = perm[...]
    device_row = target >> (rows.bit_length() - 1)
    row = target & (rows - 1)
    key = (device_row & (reps - 1)) * n + (device_row >> (reps.bit_length() - 1))
    hit = iota(i32, (count, rows), 0) == key
    hit16 = jnp.where(hit, 1.0, 0.0).astype(bf16)
    before = iota(i32, (rows, rows), 0) < iota(i32, (rows, rows), 1)
    before16 = jnp.where(before, 1.0, 0.0).astype(bf16)
    ranks = jnp.dot(hit16, before16, preferred_element_type=f32)
    rank = jnp.sum(jnp.where(hit, ranks, 0.0), axis=0, keepdims=True)
    place = key.astype(f32) * each + rank

    left_copy.wait()
    for c in range(CHUNKS):
        index = (iota(i32, (size, rows), 0) + c * size).astype(f32)
        order = jnp.where(index == place, 1.0, 0.0).astype(bf16)
        left[chunk(c)] = jnp.dot(order, raw[...], preferred_element_type=f32).astype(bf16)

    pl.semaphore_wait(barrier, count - 1)

    slot_copies = [
        remote(slots, slotv.at[a], slot_send.at[a], slot_recv.at[a], to(dests[a]))
        for a in range(ARRIVALS)
    ]
    for copy in slot_copies:
        copy.start()

    def hop(src, a, c, target):
        return remote(src, arr.at[a, chunk(c)], f_send.at[a, c], f_recv.at[a, c], to(target))

    def hop_x(c):
        return hop(left.at[chunk(c)], 0, c, px)

    def hop_y(c):
        return hop(left.at[chunk(c)], 1, c, py)

    def hop_z(c):
        return hop(arr.at[1, chunk(c)], 2, c, pz)

    def hop_far(c, a):
        return hop(arr.at[a, chunk(c)], 3, c, px)

    for c in range(CHUNKS):
        hop_y(c).start()
        hop_x(c).start()

    def key_of(d):
        return (d % reps) * n + d // reps

    shift = (me * each) % 128
    lanes = (iota(i32, (128, rows), 0) - shift).astype(f32)
    within = jnp.where(lanes == rank, 1.0, 0.0).astype(bf16)
    high = jnp.where(hit, (row >> 4).astype(f32), 0.0).astype(bf16)
    low = jnp.where(hit, (row & 15).astype(f32), 0.0).astype(bf16)
    rows_out = 16.0 * lax.dot_general(
        high, within, NT, preferred_element_type=f32
    ) + lax.dot_general(low, within, NT, preferred_element_type=f32)
    for g in range(count // 8):
        pout[g] = rows_out[8 * g : 8 * g + 8]
    pos_local = pltpu.make_async_copy(pout.at[key_of(me) // 8], pin.at[me], p_local)
    pos_local.start()

    @pl.loop(1, count)
    def _(t):
        d = (me + t) % count
        remote(pout.at[key_of(d) // 8], pin.at[me], p_send, p_recv, device(d)).start()

    cat_copy.wait()
    own_slots.wait()
    for c in range(CHUNKS):
        acc, stat = attend(left[chunk(c)], cat, lambda j: slots_sm[0, 0, j])
        own_acc[chunk(c)] = acc
        own_stat[chunk(c)] = stat

    for a in range(ARRIVALS):
        slot_copies[a].wait_recv()
        local = pltpu.make_async_copy(slotv.at[a], slots_sm.at[1 + a], slot_local.at[1 + a])
        local.start()
        local.wait()

    def back(a, c):
        return (
            remote(accs.at[a, chunk(c)], acc_in.at[a, chunk(c)], r_send.at[a, c],
                   r_recv.at[a, c], to(origins[a])),
            remote(stats.at[a, c], stat_in.at[a, c], s_send.at[a, c],
                   s_recv.at[a, c], to(origins[a])),
        )

    def serve(a, c):
        acc, stat = attend(arr[a, chunk(c)], cat, lambda j: slots_sm[1 + a, 1 + a, j])
        accs[a, chunk(c)] = acc.astype(jnp.bfloat16)
        stats[a, c] = stat.T[:8, :]
        for copy in back(a, c):
            copy.start()

    def take_y(c):
        hop_y(c).wait_recv()
        hop_z(c).start()

        @pl.when(early)
        def _():
            hop_far(c, 1).start()

    def take_z(c):
        hop_z(c).wait_recv()

        @pl.when(jnp.logical_not(early))
        def _():
            hop_far(c, 2).start()

    take_y(0)
    serve(1, 0)
    hop_x(0).wait_recv()
    serve(0, 0)
    take_y(1)
    take_z(0)
    serve(1, 1)
    serve(2, 0)
    hop_x(1).wait_recv()
    serve(0, 1)
    take_z(1)
    hop_far(0, 1).wait_recv()
    serve(3, 0)
    serve(2, 1)
    hop_far(1, 1).wait_recv()
    serve(3, 1)

    def lot(q):
        return pl.ds(pl.multiple_of(q * each, each), each)

    row_local = pltpu.make_async_copy(joined.at[lot(key_of(me))], gin.at[lot(me)], g_local)

    for c in range(CHUNKS):
        for a in range(ARRIVALS):
            for copy in back(a, c):
                copy.wait_recv()
        columns = [own_stat[chunk(c)]]
        for a in range(ARRIVALS):
            columns.append(jnp.concatenate([stat_in[a, c]] * 16, axis=0).T)
        peak = columns[0][:, 0:1]
        for column in columns[1:]:
            peak = jnp.maximum(peak, column[:, 0:1])
        factor = jnp.exp(columns[0][:, 0:1] - peak)
        numer = factor * own_acc[chunk(c)]
        denom = factor * columns[0][:, 1:2]
        for a in range(ARRIVALS):
            factor = jnp.exp(columns[1 + a][:, 0:1] - peak)
            numer = numer + factor * acc_in[a, chunk(c)].astype(jnp.float32)
            denom = denom + factor * columns[1 + a][:, 1:2]
        joined[chunk(c)] = (numer / denom).astype(jnp.bfloat16)

        def row_copy(shard):
            return remote(
                joined.at[lot(c * n + shard)], gin.at[lot(me)], g_send, g_recv,
                {"shard": shard, "rep": c},
            )

        @pl.when(rep != c)
        def _():
            row_copy(s).start()

        @pl.when(rep == c)
        def _():
            row_local.start()

        @pl.loop(1, n)
        def _(t):
            row_copy((s + t) % n).start()

    for c in range(CHUNKS):
        for a in range(ARRIVALS):
            for copy in back(a, c):
                copy.wait_send()
        hop_x(c).wait_send()
        hop_y(c).wait_send()
        hop_z(c).wait_send()
        hop_far(c, 1).wait_send()
    for copy in slot_copies:
        copy.wait_send()
    other = device((me + 1) % count)
    tiles = pin.at[pl.ds(0, count - 1)]
    pos = remote(tiles, tiles, p_send, p_recv, other)
    pos.wait_send()
    pos.wait_recv()
    pos_local.wait()
    per = 128 // each
    groups = rows // 128
    mine = iota(i32, (8, 128), 0) == key_of(me) % 8
    landing_row = iota(i32, (rows, 128), 0).astype(f32)
    spread = []
    for g in range(groups):
        tile = pin[g * per]
        for b in range(1, per):
            tile = tile + pin[g * per + b]
        landing = jnp.sum(jnp.where(mine, tile, 0.0), axis=0, keepdims=True)
        spread.append(jnp.where(landing_row == landing, 1.0, 0.0))
    spread = jnp.concatenate(spread, axis=1).astype(bf16)

    most = pl.ds(0, (count - 1) * each)
    sent = remote(joined.at[most], gin.at[most], g_send, g_recv, other)
    sent.wait_send()
    sent.wait_recv()
    row_local.wait()
    out[...] = jnp.dot(spread, gin[...], preferred_element_type=jnp.float32).astype(jnp.bfloat16)


def fused_body(left, catalog, probes, perm):
    n = lax.axis_size("shard")
    reps = lax.axis_size("rep")
    s = lax.axis_index("shard")
    rows = left.shape[0]
    count = n * reps

    py = partner_y(s)
    pyz = partner_z(py, n)
    far = jnp.where(is_early(s), partner_x(pyz), partner_x(py))
    owners = jnp.stack([s, partner_x(s), py, pyz, far])
    listed = probes[0]
    hit = (listed[None, :] >= 0) & (listed[None, :] // CB_DEV == owners[:, None])
    places = jnp.cumsum(hit.astype(jnp.int32), axis=1) - 1
    chosen = hit[:, None, :] & (places[:, None, :] == jnp.arange(CAP)[None, :, None])
    slots = jnp.max(jnp.where(chosen, listed[None, None, :] % CB_DEV, -1), axis=2)
    slots = jnp.pad(slots.astype(jnp.int32), ((0, 3), (0, 128 - CAP)))

    bf16, f32, i32 = jnp.bfloat16, jnp.float32, jnp.int32
    size = rows // CHUNKS
    dma = pltpu.SemaphoreType.DMA
    vmem = pl.BlockSpec(memory_space=pltpu.VMEM)
    return pl.pallas_call(
        functools.partial(fused_kernel, n, reps),
        out_shape=jax.ShapeDtypeStruct((rows, A), bf16),
        in_specs=[pl.BlockSpec(memory_space=pl.ANY)] * 2 + [vmem, vmem],
        out_specs=vmem,
        scratch_shapes=[
            pltpu.VMEM((rows, D), bf16),
            pltpu.VMEM((rows, D), bf16),
            pltpu.VMEM((count // 8, 8, 128), f32),
            pltpu.VMEM((CB_DEV, BLK, D + A), bf16),
            pltpu.VMEM((ARRIVALS, rows, D), bf16),
            pltpu.VMEM((ARRIVALS, 8, 128), i32),
            pltpu.SMEM((ARRIVALS + 1, 8, 128), i32),
            pltpu.VMEM((ARRIVALS, rows, A), bf16),
            pltpu.VMEM((ARRIVALS, CHUNKS, 8, size), f32),
            pltpu.VMEM((ARRIVALS, rows, A), bf16),
            pltpu.VMEM((ARRIVALS, CHUNKS, 8, size), f32),
            pltpu.VMEM((rows, A), f32),
            pltpu.VMEM((rows, 128), f32),
            pltpu.VMEM((rows, A), bf16),
            pltpu.VMEM((rows, A), bf16),
            pltpu.VMEM((count, 8, 128), f32),
            dma, dma, dma((ARRIVALS + 1,)), dma((ARRIVALS,)), dma((ARRIVALS,)),
            dma((ARRIVALS, CHUNKS)), dma((ARRIVALS, CHUNKS)),
            dma((ARRIVALS, CHUNKS)), dma((ARRIVALS, CHUNKS)),
            dma((ARRIVALS, CHUNKS)), dma((ARRIVALS, CHUNKS)),
            dma, dma, dma, dma, dma, dma,
        ],
        compiler_params=pltpu.CompilerParams(
            collective_id=0, has_side_effects=True, vmem_limit_bytes=48 * 1024 * 1024
        ),
        cost_estimate=pl.CostEstimate(
            flops=10 * rows * CAP * BLK * (D + A),
            bytes_accessed=catalog.size * 2 + rows * (D + A) * 2,
            transcendentals=5 * rows * CAP * BLK,
        ),
    )(left, catalog.reshape(CB_DEV, BLK, D + A), slots, perm.reshape(1, rows))


def body(left, catalog, probes, perm):
    n = lax.axis_size("shard")
    reps = lax.axis_size("rep")
    rows = left.shape[0]
    each = rows // (n * reps)
    if each == 16 and rows & (rows - 1) == 0 and reps == CHUNKS and n % 4 == 0 and n >= 16:
        return fused_body(left, catalog, probes, perm)
    return plain_body(left, catalog, probes, perm)


def solution(mesh):
    placed = (
        P(("shard", "rep"), None),
        P("shard", None),
        P(("shard", "rep"), None),
        P(("shard", "rep")),
    )
    return jax.shard_map(
        body, mesh=mesh, in_specs=placed, out_specs=P(("shard", "rep"), None), check_vma=False
    )
```

```python
import functools
import math

import jax
import jax.numpy as jnp
from jax import lax
from jax.experimental import pallas as pl
from jax.experimental.pallas import tpu as pltpu
from jax.sharding import PartitionSpec as P

D = 1024
A = 768
BLK = 256
CB_DEV = 8
REACH = 2
CAP = 5
SCALE = 2.5 / math.sqrt(D)
NT = (((1,), (1,)), ((), ()))


def shifted(block, axis, distance):
    devices = range(lax.axis_size(axis))
    route = [((i - distance) % len(devices), i) for i in devices]
    return lax.ppermute(block, axis, route)


def slots_for(listed, owner):
    hit = (listed >= 0) & (listed // CB_DEV == owner)
    places = jnp.cumsum(hit.astype(jnp.int32)) - 1
    chosen = hit[None, :] & (places[None, :] == jnp.arange(CAP)[:, None])
    return jnp.max(jnp.where(chosen, listed[None, :] % CB_DEV, -1), axis=1)


def group_kernel(slots_ref, q_ref, *refs):
    blocks, (acc_ref, stat_ref) = refs[:CAP], refs[CAP:]
    q = q_ref[...]
    scores = []
    for j in range(CAP):
        s = lax.dot_general(q, blocks[j][:, :D], NT, preferred_element_type=jnp.float32) * SCALE
        scores.append(jnp.where(slots_ref[j] >= 0, s, -jnp.inf))
    peak = scores[0]
    for s in scores[1:]:
        peak = jnp.maximum(peak, s)
    peak = jnp.max(peak, axis=1, keepdims=True)
    total = jnp.zeros_like(peak)
    acc = None
    for j in range(CAP):
        e = jnp.exp(scores[j] - peak)
        total = total + jnp.sum(e, axis=1, keepdims=True)
        part = jnp.dot(e.astype(jnp.bfloat16), blocks[j][:, D:], preferred_element_type=jnp.float32)
        acc = part if acc is None else acc + part
    acc_ref[...] = acc.astype(acc_ref.dtype)
    lane = lax.broadcasted_iota(jnp.int32, (q.shape[0], 128), 1)
    stat = jnp.where(lane == 0, peak, total)
    stat_ref[...] = stat.T[:8, :]


def group_partial(q, catalog, slots, dtype):
    rows = q.shape[0]
    chunk = 256
    return pl.pallas_call(
        group_kernel,
        grid_spec=pltpu.PrefetchScalarGridSpec(
            num_scalar_prefetch=1,
            grid=(rows // chunk,),
            in_specs=[pl.BlockSpec((chunk, D), lambda i, s: (i, 0))]
            + [
                pl.BlockSpec((BLK, D + A), lambda i, s, j=j: (jnp.maximum(s[j], 0), 0))
                for j in range(CAP)
            ],
            out_specs=[
                pl.BlockSpec((chunk, A), lambda i, s: (i, 0)),
                pl.BlockSpec((8, chunk), lambda i, s: (0, i)),
            ],
        ),
        out_shape=[
            jax.ShapeDtypeStruct((rows, A), dtype),
            jax.ShapeDtypeStruct((8, rows), jnp.float32),
        ],
        compiler_params=pltpu.CompilerParams(vmem_limit_bytes=40 * 1024 * 1024),
        cost_estimate=pl.CostEstimate(
            flops=2 * rows * CAP * BLK * (D + A),
            bytes_accessed=CAP * BLK * (D + A) * 2 + rows * (D + 2 * A) * 2,
            transcendentals=rows * CAP * BLK,
        ),
    )(slots, q, *([catalog] * CAP))


def plain_body(left, catalog, probes, perm):
    shard_count = lax.axis_size("shard")
    rep_count = lax.axis_size("rep")
    own = lax.axis_index("shard")
    block_rows = left.shape[0]
    devices = shard_count * rep_count
    rows_each = block_rows // devices
    offsets = (2, -2, 1, -1)
    moved = {k: shifted(left, "shard", k) for k in offsets}
    lists = {k: shifted(probes, "shard", k) for k in offsets}

    target_device = perm // block_rows
    target_row = perm % block_rows
    index = jnp.arange(block_rows)
    earlier = (target_device[:, None] == target_device[None, :]) & (index[None, :] < index[:, None])
    place = target_device * rows_each + jnp.sum(earlier.astype(jnp.int32), axis=1)
    order = place[None, :] == index[:, None]
    positions = jnp.sum(jnp.where(order, target_row[None, :], 0), axis=1).astype(jnp.int32)
    landing = lax.all_to_all(
        positions.reshape(devices, rows_each), ("shard", "rep"), 0, 0, tiled=True
    ).reshape(-1)

    parts = [group_partial(left, catalog, slots_for(probes[0], own), jnp.float32)]
    for k in offsets:
        acc, stat = group_partial(
            moved[k], catalog, slots_for(lists[k][0], own), jnp.bfloat16
        )
        parts.append((shifted(acc, "shard", -k), shifted(stat[:2], "shard", -k)))
    peak = parts[0][1][0]
    for part in parts[1:]:
        peak = jnp.maximum(peak, part[1][0])
    numer = jnp.zeros((block_rows, A), jnp.float32)
    denom = jnp.zeros((block_rows,), jnp.float32)
    for acc, stat in parts:
        factor = jnp.exp(stat[0] - peak)
        numer = numer + factor[:, None] * acc.astype(jnp.float32)
        denom = denom + factor * stat[1]
    joined = (numer / denom[:, None]).astype(jnp.bfloat16)

    outgoing = jnp.dot(
        order.astype(jnp.bfloat16), joined, preferred_element_type=jnp.float32
    ).astype(jnp.bfloat16)
    arrived = lax.all_to_all(
        outgoing.reshape(devices, rows_each, A), ("shard", "rep"), 0, 0, tiled=True
    ).reshape(block_rows, A)
    spread = (landing[None, :] == index[:, None]).astype(jnp.bfloat16)
    return jnp.dot(spread, arrived, preferred_element_type=jnp.float32).astype(jnp.bfloat16)


MESH = pl.DeviceIdType.MESH
ARRIVALS = 4
CHUNKS = 4


def partner_x(s):
    return s + 1 - 2 * (s % 2)


def partner_y(s):
    return s + 2 - 4 * ((s // 2) % 2)


def partner_z(s, n):
    return (s + 4 - 8 * ((s // 2) % 2) + n) % n


def source_z(s, n):
    return (s - 4 + 8 * ((s // 2) % 2) + n) % n


def parity(s):
    return (s + s // 2 + s // 4) % 2


def of_parity(u, p):
    return 2 * u + (p + u + u // 2) % 2


def is_early(s):
    return (s % 4) * (3 - s % 4) == 0


def attend(q, cat, slot_of):
    slots = [slot_of(j) for j in range(CAP)]
    picks = [jnp.maximum(slot, 0) for slot in slots]
    scores = []
    for j in range(CAP):
        keys = cat[picks[j], :, :D]
        s = lax.dot_general(q, keys, NT, preferred_element_type=jnp.float32) * SCALE
        scores.append(jnp.where(slots[j] >= 0, s, -jnp.inf))
    peak = scores[0]
    for s in scores[1:]:
        peak = jnp.maximum(peak, s)
    peak = jnp.max(peak, axis=1, keepdims=True)
    total = jnp.zeros_like(peak)
    acc = None
    for j in range(CAP):
        e = jnp.exp(scores[j] - peak)
        total = total + jnp.sum(e, axis=1, keepdims=True)
        values = cat[picks[j], :, D:]
        part = jnp.dot(e.astype(jnp.bfloat16), values, preferred_element_type=jnp.float32)
        acc = part if acc is None else acc + part
    lane = lax.broadcasted_iota(jnp.int32, (q.shape[0], 128), 1)
    return acc, jnp.where(lane == 0, peak, total)


def fused_kernel(
    n, reps, left_hbm, cat_hbm, slots, perm, out,
    raw, left, pout, cat, arr, slotv, slots_sm, accs, stats, acc_in, stat_in, own_acc, own_stat,
    joined, gin, pin,
    left_sem, cat_sem, slot_local, slot_send, slot_recv, f_send, f_recv,
    r_send, r_recv, s_send, s_recv, p_send, p_recv, p_local, g_send, g_recv, g_local,
):
    count = n * reps
    rows = left.shape[0]
    size = rows // CHUNKS
    each = rows // count
    s = lax.axis_index("shard")
    rep = lax.axis_index("rep")
    me = s * reps + rep
    early = is_early(s)
    px, py, pz = partner_x(s), partner_y(s), partner_z(s, n)
    pyz = partner_z(py, n)
    far = jnp.where(early, partner_x(pyz), partner_x(py))
    dests = [px, py, pyz, far]
    zs = source_z(s, n)
    xz = source_z(px, n)
    origins = [px, py, partner_y(zs), jnp.where(is_early(px), partner_y(px), partner_y(xz))]

    def to(shard):
        return {"shard": shard, "rep": rep}

    def device(d):
        return {"shard": d // reps, "rep": d % reps}

    def remote(src, dst, send, recv, target):
        return pltpu.make_async_remote_copy(
            src_ref=src, dst_ref=dst, send_sem=send, recv_sem=recv,
            device_id=target, device_id_type=MESH,
        )

    def chunk(c):
        return pl.ds(c * size, size)

    left_copy = pltpu.make_async_copy(left_hbm, raw, left_sem)
    left_copy.start()
    cat_copy = pltpu.make_async_copy(cat_hbm, cat, cat_sem)
    cat_copy.start()
    own_slots = pltpu.make_async_copy(slots, slots_sm.at[0], slot_local.at[0])
    own_slots.start()

    barrier = pltpu.get_barrier_semaphore()

    @pl.loop(1, count)
    def _(t):
        pl.semaphore_signal(
            barrier, inc=1, device_id=device((me + t) % count), device_id_type=MESH
        )

    bf16, f32, i32 = jnp.bfloat16, jnp.float32, jnp.int32
    iota = lax.broadcasted_iota
    target = perm[...]
    device_row = target >> (rows.bit_length() - 1)
    row = target & (rows - 1)
    shard_row = device_row >> (reps.bit_length() - 1)
    side = (shard_row + (shard_row >> 1) + (shard_row >> 2)) & 1
    key = (device_row & (reps - 1)) * n + side * (n // 2) + (shard_row >> 1)
    hit = iota(i32, (count, rows), 0) == key
    hit16 = jnp.where(hit, 1.0, 0.0).astype(bf16)
    before = iota(i32, (rows, rows), 0) < iota(i32, (rows, rows), 1)
    before16 = jnp.where(before, 1.0, 0.0).astype(bf16)
    ranks = jnp.dot(hit16, before16, preferred_element_type=f32)
    rank = jnp.sum(jnp.where(hit, ranks, 0.0), axis=0, keepdims=True)
    place = key.astype(f32) * each + rank

    left_copy.wait()
    for c in range(CHUNKS):
        index = (iota(i32, (size, rows), 0) + c * size).astype(f32)
        order = jnp.where(index == place, 1.0, 0.0).astype(bf16)
        left[chunk(c)] = jnp.dot(order, raw[...], preferred_element_type=f32).astype(bf16)

    pl.semaphore_wait(barrier, count - 1)

    slot_copies = [
        remote(slots, slotv.at[a], slot_send.at[a], slot_recv.at[a], to(dests[a]))
        for a in range(ARRIVALS)
    ]
    for copy in slot_copies:
        copy.start()

    def hop(src, a, c, target):
        return remote(src, arr.at[a, chunk(c)], f_send.at[a, c], f_recv.at[a, c], to(target))

    def hop_x(c):
        return hop(left.at[chunk(c)], 0, c, px)

    def hop_y(c):
        return hop(left.at[chunk(c)], 1, c, py)

    def hop_z(c):
        return hop(arr.at[1, chunk(c)], 2, c, pz)

    def hop_far(c, a):
        return hop(arr.at[a, chunk(c)], 3, c, px)

    for c in range(CHUNKS):
        hop_y(c).start()
        hop_x(c).start()

    def key_of(d):
        shard = d // reps
        return (d % reps) * n + parity(shard) * (n // 2) + shard // 2

    shift = (me * each) % 128
    lanes = (iota(i32, (128, rows), 0) - shift).astype(f32)
    within = jnp.where(lanes == rank, 1.0, 0.0).astype(bf16)
    high = jnp.where(hit, (row >> 4).astype(f32), 0.0).astype(bf16)
    low = jnp.where(hit, (row & 15).astype(f32), 0.0).astype(bf16)
    rows_out = 16.0 * lax.dot_general(
        high, within, NT, preferred_element_type=f32
    ) + lax.dot_general(low, within, NT, preferred_element_type=f32)
    for g in range(count // 8):
        pout[g] = rows_out[8 * g : 8 * g + 8]
    pos_local = pltpu.make_async_copy(pout.at[key_of(me) // 8], pin.at[me], p_local)
    pos_local.start()

    @pl.loop(1, count)
    def _(t):
        d = (me + t) % count
        remote(pout.at[key_of(d) // 8], pin.at[me], p_send, p_recv, device(d)).start()

    cat_copy.wait()
    own_slots.wait()
    for c in range(CHUNKS):
        acc, stat = attend(left[chunk(c)], cat, lambda j: slots_sm[0, 0, j])
        own_acc[chunk(c)] = acc
        own_stat[chunk(c)] = stat

    for a in range(ARRIVALS):
        slot_copies[a].wait_recv()
        local = pltpu.make_async_copy(slotv.at[a], slots_sm.at[1 + a], slot_local.at[1 + a])
        local.start()
        local.wait()

    def back(a, c):
        return (
            remote(accs.at[a, chunk(c)], acc_in.at[a, chunk(c)], r_send.at[a, c],
                   r_recv.at[a, c], to(origins[a])),
            remote(stats.at[a, c], stat_in.at[a, c], s_send.at[a, c],
                   s_recv.at[a, c], to(origins[a])),
        )

    def serve(a, c):
        acc, stat = attend(arr[a, chunk(c)], cat, lambda j: slots_sm[1 + a, 1 + a, j])
        accs[a, chunk(c)] = acc.astype(jnp.bfloat16)
        stats[a, c] = stat.T[:8, :]

    def give(a, c):
        for copy in back(a, c):
            copy.start()

    def take_y(c):
        hop_y(c).wait_recv()
        hop_z(c).start()

        @pl.when(early)
        def _():
            hop_far(c, 1).start()

    def take_z(c):
        hop_z(c).wait_recv()

        @pl.when(jnp.logical_not(early))
        def _():
            hop_far(c, 2).start()

    for c in range(CHUNKS):
        take_y(c)
        if c > 0:
            take_z(c - 1)
        serve(1, c)
        give(1, c)
        hop_x(c).wait_recv()
        serve(0, c)
        if c > 0:
            serve(2, c - 1)
            give(2, c - 1)
    last = CHUNKS - 1
    take_z(last)
    serve(2, last)
    give(2, last)
    for c in range(CHUNKS):
        hop_far(c, 1).wait_recv()
        serve(3, c)
        give(3, c)
        give(0, c)

    def lot(q):
        return pl.ds(pl.multiple_of(q * each, each), each)

    row_local = pltpu.make_async_copy(joined.at[lot(key_of(me))], gin.at[lot(me)], g_local)

    for c in range(CHUNKS):
        for a in range(ARRIVALS):
            for copy in back(a, c):
                copy.wait_recv()
        columns = [own_stat[chunk(c)]]
        for a in range(ARRIVALS):
            columns.append(jnp.concatenate([stat_in[a, c]] * 16, axis=0).T)
        peak = columns[0][:, 0:1]
        for column in columns[1:]:
            peak = jnp.maximum(peak, column[:, 0:1])
        factor = jnp.exp(columns[0][:, 0:1] - peak)
        numer = factor * own_acc[chunk(c)]
        denom = factor * columns[0][:, 1:2]
        for a in range(ARRIVALS):
            factor = jnp.exp(columns[1 + a][:, 0:1] - peak)
            numer = numer + factor * acc_in[a, chunk(c)].astype(jnp.float32)
            denom = denom + factor * columns[1 + a][:, 1:2]
        joined[chunk(c)] = (numer / denom).astype(jnp.bfloat16)

        half = n // 2
        here = (rep - c // 2) * (rep - c // 2) + (parity(s) - c % 2) * (parity(s) - c % 2) == 0

        def row_copy(t):
            u = (s // 2 + t) % half
            return remote(
                joined.at[lot(c * half + u)], gin.at[lot(me)], g_send, g_recv,
                {"shard": of_parity(u, c % 2), "rep": c // 2},
            )

        @pl.when(jnp.logical_not(here))
        def _():
            row_copy(0).start()

        @pl.when(here)
        def _():
            row_local.start()

        @pl.loop(1, half)
        def _(t):
            row_copy(t).start()

    for c in range(CHUNKS):
        for a in range(ARRIVALS):
            for copy in back(a, c):
                copy.wait_send()
        hop_x(c).wait_send()
        hop_y(c).wait_send()
        hop_z(c).wait_send()
        hop_far(c, 1).wait_send()
    for copy in slot_copies:
        copy.wait_send()
    other = device((me + 1) % count)
    tiles = pin.at[pl.ds(0, count - 1)]
    pos = remote(tiles, tiles, p_send, p_recv, other)
    pos.wait_send()
    pos.wait_recv()
    pos_local.wait()
    per = 128 // each
    groups = rows // 128
    mine = iota(i32, (8, 128), 0) == key_of(me) % 8
    landing_row = iota(i32, (rows, 128), 0).astype(f32)
    spread = []
    for g in range(groups):
        tile = pin[g * per]
        for b in range(1, per):
            tile = tile + pin[g * per + b]
        landing = jnp.sum(jnp.where(mine, tile, 0.0), axis=0, keepdims=True)
        spread.append(jnp.where(landing_row == landing, 1.0, 0.0))
    spread = jnp.concatenate(spread, axis=1).astype(bf16)

    most = pl.ds(0, (count - 1) * each)
    sent = remote(joined.at[most], gin.at[most], g_send, g_recv, other)
    sent.wait_send()
    sent.wait_recv()
    row_local.wait()
    out[...] = jnp.dot(spread, gin[...], preferred_element_type=jnp.float32).astype(jnp.bfloat16)


def fused_body(left, catalog, probes, perm):
    n = lax.axis_size("shard")
    reps = lax.axis_size("rep")
    s = lax.axis_index("shard")
    rows = left.shape[0]
    count = n * reps

    py = partner_y(s)
    pyz = partner_z(py, n)
    far = jnp.where(is_early(s), partner_x(pyz), partner_x(py))
    owners = jnp.stack([s, partner_x(s), py, pyz, far])
    listed = probes[0]
    hit = (listed[None, :] >= 0) & (listed[None, :] // CB_DEV == owners[:, None])
    places = jnp.cumsum(hit.astype(jnp.int32), axis=1) - 1
    chosen = hit[:, None, :] & (places[:, None, :] == jnp.arange(CAP)[None, :, None])
    slots = jnp.max(jnp.where(chosen, listed[None, None, :] % CB_DEV, -1), axis=2)
    slots = jnp.pad(slots.astype(jnp.int32), ((0, 3), (0, 128 - CAP)))

    bf16, f32, i32 = jnp.bfloat16, jnp.float32, jnp.int32
    size = rows // CHUNKS
    dma = pltpu.SemaphoreType.DMA
    vmem = pl.BlockSpec(memory_space=pltpu.VMEM)
    return pl.pallas_call(
        functools.partial(fused_kernel, n, reps),
        out_shape=jax.ShapeDtypeStruct((rows, A), bf16),
        in_specs=[pl.BlockSpec(memory_space=pl.ANY)] * 2 + [vmem, vmem],
        out_specs=vmem,
        scratch_shapes=[
            pltpu.VMEM((rows, D), bf16),
            pltpu.VMEM((rows, D), bf16),
            pltpu.VMEM((count // 8, 8, 128), f32),
            pltpu.VMEM((CB_DEV, BLK, D + A), bf16),
            pltpu.VMEM((ARRIVALS, rows, D), bf16),
            pltpu.VMEM((ARRIVALS, 8, 128), i32),
            pltpu.SMEM((ARRIVALS + 1, 8, 128), i32),
            pltpu.VMEM((ARRIVALS, rows, A), bf16),
            pltpu.VMEM((ARRIVALS, CHUNKS, 8, size), f32),
            pltpu.VMEM((ARRIVALS, rows, A), bf16),
            pltpu.VMEM((ARRIVALS, CHUNKS, 8, size), f32),
            pltpu.VMEM((rows, A), f32),
            pltpu.VMEM((rows, 128), f32),
            pltpu.VMEM((rows, A), bf16),
            pltpu.VMEM((rows, A), bf16),
            pltpu.VMEM((count, 8, 128), f32),
            dma, dma, dma((ARRIVALS + 1,)), dma((ARRIVALS,)), dma((ARRIVALS,)),
            dma((ARRIVALS, CHUNKS)), dma((ARRIVALS, CHUNKS)),
            dma((ARRIVALS, CHUNKS)), dma((ARRIVALS, CHUNKS)),
            dma((ARRIVALS, CHUNKS)), dma((ARRIVALS, CHUNKS)),
            dma, dma, dma, dma, dma, dma,
        ],
        compiler_params=pltpu.CompilerParams(
            collective_id=0, has_side_effects=True, vmem_limit_bytes=60 * 1024 * 1024
        ),
        cost_estimate=pl.CostEstimate(
            flops=10 * rows * CAP * BLK * (D + A),
            bytes_accessed=catalog.size * 2 + rows * (D + A) * 2,
            transcendentals=5 * rows * CAP * BLK,
        ),
    )(left, catalog.reshape(CB_DEV, BLK, D + A), slots, perm.reshape(1, rows))


def body(left, catalog, probes, perm):
    n = lax.axis_size("shard")
    reps = lax.axis_size("rep")
    rows = left.shape[0]
    each = rows // (n * reps)
    if each == 16 and rows & (rows - 1) == 0 and 2 * reps == CHUNKS and n % 4 == 0 and n >= 16:
        return fused_body(left, catalog, probes, perm)
    return plain_body(left, catalog, probes, perm)


def solution(mesh):
    placed = (
        P(("shard", "rep"), None),
        P("shard", None),
        P(("shard", "rep"), None),
        P(("shard", "rep")),
    )
    return jax.shard_map(
        body, mesh=mesh, in_specs=placed, out_specs=P(("shard", "rep"), None), check_vma=False
    )
```

```python
import functools
import math

import jax
import jax.numpy as jnp
from jax import lax
from jax.experimental import pallas as pl
from jax.experimental.pallas import tpu as pltpu
from jax.sharding import PartitionSpec as P

D = 1024
A = 768
BLK = 256
CB_DEV = 8
REACH = 2
CAP = 5
SCALE = 2.5 / math.sqrt(D)
NT = (((1,), (1,)), ((), ()))


def shifted(block, axis, distance):
    devices = range(lax.axis_size(axis))
    route = [((i - distance) % len(devices), i) for i in devices]
    return lax.ppermute(block, axis, route)


def slots_for(listed, owner):
    hit = (listed >= 0) & (listed // CB_DEV == owner)
    places = jnp.cumsum(hit.astype(jnp.int32)) - 1
    chosen = hit[None, :] & (places[None, :] == jnp.arange(CAP)[:, None])
    return jnp.max(jnp.where(chosen, listed[None, :] % CB_DEV, -1), axis=1)


def group_kernel(slots_ref, q_ref, *refs):
    blocks, (acc_ref, stat_ref) = refs[:CAP], refs[CAP:]
    q = q_ref[...]
    scores = []
    for j in range(CAP):
        s = lax.dot_general(q, blocks[j][:, :D], NT, preferred_element_type=jnp.float32) * SCALE
        scores.append(jnp.where(slots_ref[j] >= 0, s, -jnp.inf))
    peak = scores[0]
    for s in scores[1:]:
        peak = jnp.maximum(peak, s)
    peak = jnp.max(peak, axis=1, keepdims=True)
    total = jnp.zeros_like(peak)
    acc = None
    for j in range(CAP):
        e = jnp.exp(scores[j] - peak)
        total = total + jnp.sum(e, axis=1, keepdims=True)
        part = jnp.dot(e.astype(jnp.bfloat16), blocks[j][:, D:], preferred_element_type=jnp.float32)
        acc = part if acc is None else acc + part
    acc_ref[...] = acc.astype(acc_ref.dtype)
    lane = lax.broadcasted_iota(jnp.int32, (q.shape[0], 128), 1)
    stat = jnp.where(lane == 0, peak, total)
    stat_ref[...] = stat.T[:8, :]


def group_partial(q, catalog, slots, dtype):
    rows = q.shape[0]
    chunk = 256
    return pl.pallas_call(
        group_kernel,
        grid_spec=pltpu.PrefetchScalarGridSpec(
            num_scalar_prefetch=1,
            grid=(rows // chunk,),
            in_specs=[pl.BlockSpec((chunk, D), lambda i, s: (i, 0))]
            + [
                pl.BlockSpec((BLK, D + A), lambda i, s, j=j: (jnp.maximum(s[j], 0), 0))
                for j in range(CAP)
            ],
            out_specs=[
                pl.BlockSpec((chunk, A), lambda i, s: (i, 0)),
                pl.BlockSpec((8, chunk), lambda i, s: (0, i)),
            ],
        ),
        out_shape=[
            jax.ShapeDtypeStruct((rows, A), dtype),
            jax.ShapeDtypeStruct((8, rows), jnp.float32),
        ],
        compiler_params=pltpu.CompilerParams(vmem_limit_bytes=40 * 1024 * 1024),
        cost_estimate=pl.CostEstimate(
            flops=2 * rows * CAP * BLK * (D + A),
            bytes_accessed=CAP * BLK * (D + A) * 2 + rows * (D + 2 * A) * 2,
            transcendentals=rows * CAP * BLK,
        ),
    )(slots, q, *([catalog] * CAP))


def plain_body(left, catalog, probes, perm):
    shard_count = lax.axis_size("shard")
    rep_count = lax.axis_size("rep")
    own = lax.axis_index("shard")
    block_rows = left.shape[0]
    devices = shard_count * rep_count
    rows_each = block_rows // devices
    offsets = (2, -2, 1, -1)
    moved = {k: shifted(left, "shard", k) for k in offsets}
    lists = {k: shifted(probes, "shard", k) for k in offsets}

    target_device = perm // block_rows
    target_row = perm % block_rows
    index = jnp.arange(block_rows)
    earlier = (target_device[:, None] == target_device[None, :]) & (index[None, :] < index[:, None])
    place = target_device * rows_each + jnp.sum(earlier.astype(jnp.int32), axis=1)
    order = place[None, :] == index[:, None]
    positions = jnp.sum(jnp.where(order, target_row[None, :], 0), axis=1).astype(jnp.int32)
    landing = lax.all_to_all(
        positions.reshape(devices, rows_each), ("shard", "rep"), 0, 0, tiled=True
    ).reshape(-1)

    parts = [group_partial(left, catalog, slots_for(probes[0], own), jnp.float32)]
    for k in offsets:
        acc, stat = group_partial(
            moved[k], catalog, slots_for(lists[k][0], own), jnp.bfloat16
        )
        parts.append((shifted(acc, "shard", -k), shifted(stat[:2], "shard", -k)))
    peak = parts[0][1][0]
    for part in parts[1:]:
        peak = jnp.maximum(peak, part[1][0])
    numer = jnp.zeros((block_rows, A), jnp.float32)
    denom = jnp.zeros((block_rows,), jnp.float32)
    for acc, stat in parts:
        factor = jnp.exp(stat[0] - peak)
        numer = numer + factor[:, None] * acc.astype(jnp.float32)
        denom = denom + factor * stat[1]
    joined = (numer / denom[:, None]).astype(jnp.bfloat16)

    outgoing = jnp.dot(
        order.astype(jnp.bfloat16), joined, preferred_element_type=jnp.float32
    ).astype(jnp.bfloat16)
    arrived = lax.all_to_all(
        outgoing.reshape(devices, rows_each, A), ("shard", "rep"), 0, 0, tiled=True
    ).reshape(block_rows, A)
    spread = (landing[None, :] == index[:, None]).astype(jnp.bfloat16)
    return jnp.dot(spread, arrived, preferred_element_type=jnp.float32).astype(jnp.bfloat16)


MESH = pl.DeviceIdType.MESH
ARRIVALS = 4
CHUNKS = 4


def partner_x(s):
    return s + 1 - 2 * (s % 2)


def partner_y(s):
    return s + 2 - 4 * ((s // 2) % 2)


def partner_z(s, n):
    return (s + 4 - 8 * ((s // 2) % 2) + n) % n


def source_z(s, n):
    return (s - 4 + 8 * ((s // 2) % 2) + n) % n


def parity(s):
    return (s + s // 2 + s // 4) % 2


def of_parity(u, p):
    return 2 * u + (p + u + u // 2) % 2


def is_early(s):
    return (s % 4) * (3 - s % 4) == 0


def attend(q, cat, slot_of):
    slots = [slot_of(j) for j in range(CAP)]
    picks = [jnp.maximum(slot, 0) for slot in slots]
    scores = []
    for j in range(CAP):
        keys = cat[picks[j], :, :D]
        s = lax.dot_general(q, keys, NT, preferred_element_type=jnp.float32) * SCALE
        scores.append(jnp.where(slots[j] >= 0, s, -jnp.inf))
    peak = scores[0]
    for s in scores[1:]:
        peak = jnp.maximum(peak, s)
    peak = jnp.max(peak, axis=1, keepdims=True)
    total = jnp.zeros_like(peak)
    acc = None
    for j in range(CAP):
        e = jnp.exp(scores[j] - peak)
        total = total + jnp.sum(e, axis=1, keepdims=True)
        values = cat[picks[j], :, D:]
        part = jnp.dot(e.astype(jnp.bfloat16), values, preferred_element_type=jnp.float32)
        acc = part if acc is None else acc + part
    lane = lax.broadcasted_iota(jnp.int32, (q.shape[0], 128), 1)
    return acc, jnp.where(lane == 0, peak, total)


def fused_kernel(
    n, reps, left_hbm, cat_hbm, slots, perm, out,
    raw, left, pout, cat, arr, slotv, slots_sm, accs, stats, acc_in, stat_in, own_acc, own_stat,
    joined, gin, pin,
    left_sem, cat_sem, slot_local, slot_send, slot_recv, f_send, f_recv,
    r_send, r_recv, s_send, s_recv, p_send, p_recv, p_local, g_send, g_recv, g_local,
):
    count = n * reps
    rows = left.shape[0]
    size = rows // CHUNKS
    each = rows // count
    s = lax.axis_index("shard")
    rep = lax.axis_index("rep")
    me = s * reps + rep
    early = is_early(s)
    px, py, pz = partner_x(s), partner_y(s), partner_z(s, n)
    pyz = partner_z(py, n)
    far = jnp.where(early, partner_x(pyz), partner_x(py))
    dests = [px, py, pyz, far]
    zs = source_z(s, n)
    xz = source_z(px, n)
    pfar = (s + 2 - 4 * (s % 2) + n) % n
    meets = [partner_y(px), py, zs, jnp.where(is_early(px), px, xz)]
    source = py * reps + rep

    def to(shard):
        return {"shard": shard, "rep": rep}

    def device(d):
        return {"shard": d // reps, "rep": d % reps}

    def remote(src, dst, send, recv, target):
        return pltpu.make_async_remote_copy(
            src_ref=src, dst_ref=dst, send_sem=send, recv_sem=recv,
            device_id=target, device_id_type=MESH,
        )

    def chunk(c):
        return pl.ds(c * size, size)

    left_copy = pltpu.make_async_copy(left_hbm, raw, left_sem)
    left_copy.start()
    cat_copy = pltpu.make_async_copy(cat_hbm, cat, cat_sem)
    cat_copy.start()
    own_slots = pltpu.make_async_copy(slots, slots_sm.at[0], slot_local.at[0])
    own_slots.start()

    barrier = pltpu.get_barrier_semaphore()

    @pl.loop(1, count)
    def _(t):
        pl.semaphore_signal(
            barrier, inc=1, device_id=device((me + t) % count), device_id_type=MESH
        )

    bf16, f32, i32 = jnp.bfloat16, jnp.float32, jnp.int32
    iota = lax.broadcasted_iota
    target = perm[...]
    device_row = target >> (rows.bit_length() - 1)
    row = target & (rows - 1)
    shard_row = device_row >> (reps.bit_length() - 1)
    side = (shard_row + (shard_row >> 1) + (shard_row >> 2)) & 1
    key = (device_row & (reps - 1)) * n + side * (n // 2) + (shard_row >> 1)
    hit = iota(i32, (count, rows), 0) == key
    hit16 = jnp.where(hit, 1.0, 0.0).astype(bf16)
    before = iota(i32, (rows, rows), 0) < iota(i32, (rows, rows), 1)
    before16 = jnp.where(before, 1.0, 0.0).astype(bf16)
    ranks = jnp.dot(hit16, before16, preferred_element_type=f32)
    rank = jnp.sum(jnp.where(hit, ranks, 0.0), axis=0, keepdims=True)
    place = key.astype(f32) * each + rank

    left_copy.wait()
    for c in range(CHUNKS):
        index = (iota(i32, (size, rows), 0) + c * size).astype(f32)
        order = jnp.where(index == place, 1.0, 0.0).astype(bf16)
        left[chunk(c)] = jnp.dot(order, raw[...], preferred_element_type=f32).astype(bf16)

    pl.semaphore_wait(barrier, count - 1)

    slot_copies = [
        remote(slots, slotv.at[a], slot_send.at[a], slot_recv.at[a], to(dests[a]))
        for a in range(ARRIVALS)
    ]
    for copy in slot_copies:
        copy.start()

    def hop(src, a, c, target):
        return remote(src, arr.at[a, chunk(c)], f_send.at[a, c], f_recv.at[a, c], to(target))

    def hop_x(c):
        return hop(left.at[chunk(c)], 0, c, px)

    def hop_y(c):
        return hop(left.at[chunk(c)], 1, c, py)

    def hop_z(c):
        return hop(arr.at[1, chunk(c)], 2, c, pz)

    def hop_far(c, a, target):
        return hop(arr.at[a, chunk(c)], 3, c, target)

    for c in range(CHUNKS):
        hop_y(c).start()
        hop_x(c).start()

    def key_of(d):
        shard = d // reps
        return (d % reps) * n + parity(shard) * (n // 2) + shard // 2

    shift = (me * each) % 128
    lanes = (iota(i32, (128, rows), 0) - shift).astype(f32)
    within = jnp.where(lanes == rank, 1.0, 0.0).astype(bf16)
    high = jnp.where(hit, (row >> 4).astype(f32), 0.0).astype(bf16)
    low = jnp.where(hit, (row & 15).astype(f32), 0.0).astype(bf16)
    rows_out = 16.0 * lax.dot_general(
        high, within, NT, preferred_element_type=f32
    ) + lax.dot_general(low, within, NT, preferred_element_type=f32)
    for g in range(count // 8):
        pout[g] = rows_out[8 * g : 8 * g + 8]
    pos_local = pltpu.make_async_copy(pout.at[key_of(me) // 8], pin.at[me], p_local)
    pos_local.start()

    @pl.loop(1, count)
    def _(t):
        d = (me + t) % count
        remote(pout.at[key_of(d) // 8], pin.at[me], p_send, p_recv, device(d)).start()

    def back(a, c):
        return (
            remote(accs.at[a, chunk(c)], acc_in.at[a, chunk(c)], r_send.at[a, c],
                   r_recv.at[a, c], to(meets[a])),
            remote(stats.at[a, c], stat_in.at[a, c], s_send.at[a, c],
                   s_recv.at[a, c], to(meets[a])),
        )

    def send_off(a, c, acc, stat):
        accs[a, chunk(c)] = acc.astype(jnp.bfloat16)
        stats[a, c] = stat.T[:8, :]

    cat_copy.wait()
    own_slots.wait()
    for c in range(CHUNKS):
        send_off(1, c, *attend(left[chunk(c)], cat, lambda j: slots_sm[0, 0, j]))

    for a in range(ARRIVALS):
        slot_copies[a].wait_recv()
        local = pltpu.make_async_copy(slotv.at[a], slots_sm.at[1 + a], slot_local.at[1 + a])
        local.start()
        local.wait()

    def serve(a, c):
        acc, stat = attend(arr[a, chunk(c)], cat, lambda j: slots_sm[1 + a, 1 + a, j])
        if a == 1:
            own_acc[chunk(c)] = acc
            own_stat[chunk(c)] = stat
        else:
            send_off(a, c, acc, stat)

    def give(a, c):
        for copy in back(a, c):
            copy.start()

    def by_x(c):
        return c % 2 == 0

    def take_y(c):
        hop_y(c).wait_recv()
        hop_z(c).start()
        if by_x(c):

            @pl.when(early)
            def _():
                hop_far(c, 1, px).start()

    def take_x(c):
        hop_x(c).wait_recv()
        if not by_x(c):
            hop_far(c, 0, pfar).start()

    def take_z(c):
        hop_z(c).wait_recv()
        if by_x(c):

            @pl.when(jnp.logical_not(early))
            def _():
                hop_far(c, 2, px).start()

    for c in range(CHUNKS):
        take_y(c)
        take_x(c)
        if c > 0:
            take_z(c - 1)
        serve(1, c)
        serve(0, c)
        if c > 0:
            serve(2, c - 1)
            give(2, c - 1)
    last = CHUNKS - 1
    take_z(last)
    serve(2, last)
    give(2, last)
    for c in range(CHUNKS):
        hop_far(c, 1, px).wait_recv()
        serve(3, c)
        give(3, c)
        give(0, c)
        give(1, c)

    def lot(q):
        return pl.ds(pl.multiple_of(q * each, each), each)

    row_local = pltpu.make_async_copy(joined.at[lot(key_of(me))], gin.at[lot(source)], g_local)

    for c in range(CHUNKS):
        for a in range(ARRIVALS):
            for copy in back(a, c):
                copy.wait_recv()
        columns = [own_stat[chunk(c)]]
        for a in range(ARRIVALS):
            columns.append(jnp.concatenate([stat_in[a, c]] * 16, axis=0).T)
        peak = columns[0][:, 0:1]
        for column in columns[1:]:
            peak = jnp.maximum(peak, column[:, 0:1])
        factor = jnp.exp(columns[0][:, 0:1] - peak)
        numer = factor * own_acc[chunk(c)]
        denom = factor * columns[0][:, 1:2]
        for a in range(ARRIVALS):
            factor = jnp.exp(columns[1 + a][:, 0:1] - peak)
            numer = numer + factor * acc_in[a, chunk(c)].astype(jnp.float32)
            denom = denom + factor * columns[1 + a][:, 1:2]
        joined[chunk(c)] = (numer / denom).astype(jnp.bfloat16)

        half = n // 2
        here = (rep - c // 2) * (rep - c // 2) + (parity(s) - c % 2) * (parity(s) - c % 2) == 0

        def row_copy(t):
            u = (s // 2 + t) % half
            return remote(
                joined.at[lot(c * half + u)], gin.at[lot(source)], g_send, g_recv,
                {"shard": of_parity(u, c % 2), "rep": c // 2},
            )

        @pl.when(jnp.logical_not(here))
        def _():
            row_copy(0).start()

        @pl.when(here)
        def _():
            row_local.start()

        @pl.loop(1, half)
        def _(t):
            row_copy(t).start()

    for c in range(CHUNKS):
        for a in range(ARRIVALS):
            for copy in back(a, c):
                copy.wait_send()
        hop_x(c).wait_send()
        hop_y(c).wait_send()
        hop_z(c).wait_send()
        hop_far(c, 1, px).wait_send()
    for copy in slot_copies:
        copy.wait_send()
    other = device((me + 1) % count)
    tiles = pin.at[pl.ds(0, count - 1)]
    pos = remote(tiles, tiles, p_send, p_recv, other)
    pos.wait_send()
    pos.wait_recv()
    pos_local.wait()
    per = 128 // each
    groups = rows // 128
    mine = iota(i32, (8, 128), 0) == key_of(me) % 8
    landing_row = iota(i32, (rows, 128), 0).astype(f32)
    spread = []
    for g in range(groups):
        tile = pin[g * per]
        for b in range(1, per):
            tile = tile + pin[g * per + b]
        landing = jnp.sum(jnp.where(mine, tile, 0.0), axis=0, keepdims=True)
        spread.append(jnp.where(landing_row == landing, 1.0, 0.0))
    spread = jnp.concatenate(spread, axis=1).astype(bf16)

    most = pl.ds(0, (count - 1) * each)
    sent = remote(joined.at[most], gin.at[most], g_send, g_recv, other)
    sent.wait_send()
    sent.wait_recv()
    row_local.wait()
    out[...] = jnp.dot(spread, gin[...], preferred_element_type=jnp.float32).astype(jnp.bfloat16)


def fused_body(left, catalog, probes, perm):
    n = lax.axis_size("shard")
    reps = lax.axis_size("rep")
    s = lax.axis_index("shard")
    rows = left.shape[0]
    count = n * reps

    py = partner_y(s)
    pyz = partner_z(py, n)
    far = jnp.where(is_early(s), partner_x(pyz), partner_x(py))
    owners = jnp.stack([s, partner_x(s), py, pyz, far])
    listed = probes[0]
    hit = (listed[None, :] >= 0) & (listed[None, :] // CB_DEV == owners[:, None])
    places = jnp.cumsum(hit.astype(jnp.int32), axis=1) - 1
    chosen = hit[:, None, :] & (places[:, None, :] == jnp.arange(CAP)[None, :, None])
    slots = jnp.max(jnp.where(chosen, listed[None, None, :] % CB_DEV, -1), axis=2)
    slots = jnp.pad(slots.astype(jnp.int32), ((0, 3), (0, 128 - CAP)))

    bf16, f32, i32 = jnp.bfloat16, jnp.float32, jnp.int32
    size = rows // CHUNKS
    dma = pltpu.SemaphoreType.DMA
    vmem = pl.BlockSpec(memory_space=pltpu.VMEM)
    return pl.pallas_call(
        functools.partial(fused_kernel, n, reps),
        out_shape=jax.ShapeDtypeStruct((rows, A), bf16),
        in_specs=[pl.BlockSpec(memory_space=pl.ANY)] * 2 + [vmem, vmem],
        out_specs=vmem,
        scratch_shapes=[
            pltpu.VMEM((rows, D), bf16),
            pltpu.VMEM((rows, D), bf16),
            pltpu.VMEM((count // 8, 8, 128), f32),
            pltpu.VMEM((CB_DEV, BLK, D + A), bf16),
            pltpu.VMEM((ARRIVALS, rows, D), bf16),
            pltpu.VMEM((ARRIVALS, 8, 128), i32),
            pltpu.SMEM((ARRIVALS + 1, 8, 128), i32),
            pltpu.VMEM((ARRIVALS, rows, A), bf16),
            pltpu.VMEM((ARRIVALS, CHUNKS, 8, size), f32),
            pltpu.VMEM((ARRIVALS, rows, A), bf16),
            pltpu.VMEM((ARRIVALS, CHUNKS, 8, size), f32),
            pltpu.VMEM((rows, A), f32),
            pltpu.VMEM((rows, 128), f32),
            pltpu.VMEM((rows, A), bf16),
            pltpu.VMEM((rows, A), bf16),
            pltpu.VMEM((count, 8, 128), f32),
            dma, dma, dma((ARRIVALS + 1,)), dma((ARRIVALS,)), dma((ARRIVALS,)),
            dma((ARRIVALS, CHUNKS)), dma((ARRIVALS, CHUNKS)),
            dma((ARRIVALS, CHUNKS)), dma((ARRIVALS, CHUNKS)),
            dma((ARRIVALS, CHUNKS)), dma((ARRIVALS, CHUNKS)),
            dma, dma, dma, dma, dma, dma,
        ],
        compiler_params=pltpu.CompilerParams(
            collective_id=0, has_side_effects=True, vmem_limit_bytes=60 * 1024 * 1024
        ),
        cost_estimate=pl.CostEstimate(
            flops=10 * rows * CAP * BLK * (D + A),
            bytes_accessed=catalog.size * 2 + rows * (D + A) * 2,
            transcendentals=5 * rows * CAP * BLK,
        ),
    )(left, catalog.reshape(CB_DEV, BLK, D + A), slots, perm.reshape(1, rows))


def body(left, catalog, probes, perm):
    n = lax.axis_size("shard")
    reps = lax.axis_size("rep")
    rows = left.shape[0]
    each = rows // (n * reps)
    if each == 16 and rows & (rows - 1) == 0 and 2 * reps == CHUNKS and n % 4 == 0 and n >= 16:
        return fused_body(left, catalog, probes, perm)
    return plain_body(left, catalog, probes, perm)


def solution(mesh):
    placed = (
        P(("shard", "rep"), None),
        P("shard", None),
        P(("shard", "rep"), None),
        P(("shard", "rep")),
    )
    return jax.shard_map(
        body, mesh=mesh, in_specs=placed, out_specs=P(("shard", "rep"), None), check_vma=False
    )
```

```python
import functools
import math

import jax
import jax.numpy as jnp
from jax import lax
from jax.experimental import pallas as pl
from jax.experimental.pallas import tpu as pltpu
from jax.sharding import PartitionSpec as P

D = 1024
A = 768
BLK = 256
CB_DEV = 8
REACH = 2
CAP = 5
SCALE = 2.5 / math.sqrt(D)
NT = (((1,), (1,)), ((), ()))


def shifted(block, axis, distance):
    devices = range(lax.axis_size(axis))
    route = [((i - distance) % len(devices), i) for i in devices]
    return lax.ppermute(block, axis, route)


def slots_for(listed, owner):
    hit = (listed >= 0) & (listed // CB_DEV == owner)
    places = jnp.cumsum(hit.astype(jnp.int32)) - 1
    chosen = hit[None, :] & (places[None, :] == jnp.arange(CAP)[:, None])
    return jnp.max(jnp.where(chosen, listed[None, :] % CB_DEV, -1), axis=1)


def group_kernel(slots_ref, q_ref, *refs):
    blocks, (acc_ref, stat_ref) = refs[:CAP], refs[CAP:]
    q = q_ref[...]
    scores = []
    for j in range(CAP):
        s = lax.dot_general(q, blocks[j][:, :D], NT, preferred_element_type=jnp.float32) * SCALE
        scores.append(jnp.where(slots_ref[j] >= 0, s, -jnp.inf))
    peak = scores[0]
    for s in scores[1:]:
        peak = jnp.maximum(peak, s)
    peak = jnp.max(peak, axis=1, keepdims=True)
    total = jnp.zeros_like(peak)
    acc = None
    for j in range(CAP):
        e = jnp.exp(scores[j] - peak)
        total = total + jnp.sum(e, axis=1, keepdims=True)
        part = jnp.dot(e.astype(jnp.bfloat16), blocks[j][:, D:], preferred_element_type=jnp.float32)
        acc = part if acc is None else acc + part
    acc_ref[...] = acc.astype(acc_ref.dtype)
    lane = lax.broadcasted_iota(jnp.int32, (q.shape[0], 128), 1)
    stat = jnp.where(lane == 0, peak, total)
    stat_ref[...] = stat.T[:8, :]


def group_partial(q, catalog, slots, dtype):
    rows = q.shape[0]
    chunk = 256
    return pl.pallas_call(
        group_kernel,
        grid_spec=pltpu.PrefetchScalarGridSpec(
            num_scalar_prefetch=1,
            grid=(rows // chunk,),
            in_specs=[pl.BlockSpec((chunk, D), lambda i, s: (i, 0))]
            + [
                pl.BlockSpec((BLK, D + A), lambda i, s, j=j: (jnp.maximum(s[j], 0), 0))
                for j in range(CAP)
            ],
            out_specs=[
                pl.BlockSpec((chunk, A), lambda i, s: (i, 0)),
                pl.BlockSpec((8, chunk), lambda i, s: (0, i)),
            ],
        ),
        out_shape=[
            jax.ShapeDtypeStruct((rows, A), dtype),
            jax.ShapeDtypeStruct((8, rows), jnp.float32),
        ],
        compiler_params=pltpu.CompilerParams(vmem_limit_bytes=40 * 1024 * 1024),
        cost_estimate=pl.CostEstimate(
            flops=2 * rows * CAP * BLK * (D + A),
            bytes_accessed=CAP * BLK * (D + A) * 2 + rows * (D + 2 * A) * 2,
            transcendentals=rows * CAP * BLK,
        ),
    )(slots, q, *([catalog] * CAP))


def plain_body(left, catalog, probes, perm):
    shard_count = lax.axis_size("shard")
    rep_count = lax.axis_size("rep")
    own = lax.axis_index("shard")
    block_rows = left.shape[0]
    devices = shard_count * rep_count
    rows_each = block_rows // devices
    offsets = (2, -2, 1, -1)
    moved = {k: shifted(left, "shard", k) for k in offsets}
    lists = {k: shifted(probes, "shard", k) for k in offsets}

    target_device = perm // block_rows
    target_row = perm % block_rows
    index = jnp.arange(block_rows)
    earlier = (target_device[:, None] == target_device[None, :]) & (index[None, :] < index[:, None])
    place = target_device * rows_each + jnp.sum(earlier.astype(jnp.int32), axis=1)
    order = place[None, :] == index[:, None]
    positions = jnp.sum(jnp.where(order, target_row[None, :], 0), axis=1).astype(jnp.int32)
    landing = lax.all_to_all(
        positions.reshape(devices, rows_each), ("shard", "rep"), 0, 0, tiled=True
    ).reshape(-1)

    parts = [group_partial(left, catalog, slots_for(probes[0], own), jnp.float32)]
    for k in offsets:
        acc, stat = group_partial(
            moved[k], catalog, slots_for(lists[k][0], own), jnp.bfloat16
        )
        parts.append((shifted(acc, "shard", -k), shifted(stat[:2], "shard", -k)))
    peak = parts[0][1][0]
    for part in parts[1:]:
        peak = jnp.maximum(peak, part[1][0])
    numer = jnp.zeros((block_rows, A), jnp.float32)
    denom = jnp.zeros((block_rows,), jnp.float32)
    for acc, stat in parts:
        factor = jnp.exp(stat[0] - peak)
        numer = numer + factor[:, None] * acc.astype(jnp.float32)
        denom = denom + factor * stat[1]
    joined = (numer / denom[:, None]).astype(jnp.bfloat16)

    outgoing = jnp.dot(
        order.astype(jnp.bfloat16), joined, preferred_element_type=jnp.float32
    ).astype(jnp.bfloat16)
    arrived = lax.all_to_all(
        outgoing.reshape(devices, rows_each, A), ("shard", "rep"), 0, 0, tiled=True
    ).reshape(block_rows, A)
    spread = (landing[None, :] == index[:, None]).astype(jnp.bfloat16)
    return jnp.dot(spread, arrived, preferred_element_type=jnp.float32).astype(jnp.bfloat16)


MESH = pl.DeviceIdType.MESH
ARRIVALS = 4
CHUNKS = 4
UNITS = 2


def partner_x(s):
    return s + 1 - 2 * (s % 2)


def partner_y(s):
    return s + 2 - 4 * ((s // 2) % 2)


def partner_z(s, n):
    return (s + 4 - 8 * ((s // 2) % 2) + n) % n


def source_z(s, n):
    return (s - 4 + 8 * ((s // 2) % 2) + n) % n


def parity(s):
    return (s + s // 2 + s // 4) % 2


def of_parity(u, p):
    return 2 * u + (p + u + u // 2) % 2


def is_early(s):
    return (s % 4) * (3 - s % 4) == 0


def attend(q, cat, slot_of):
    slots = [slot_of(j) for j in range(CAP)]
    picks = [jnp.maximum(slot, 0) for slot in slots]
    scores = []
    for j in range(CAP):
        keys = cat[picks[j], :, :D]
        s = lax.dot_general(q, keys, NT, preferred_element_type=jnp.float32) * SCALE
        scores.append(jnp.where(slots[j] >= 0, s, -jnp.inf))
    peak = scores[0]
    for s in scores[1:]:
        peak = jnp.maximum(peak, s)
    peak = jnp.max(peak, axis=1, keepdims=True)
    total = jnp.zeros_like(peak)
    acc = None
    for j in range(CAP):
        e = jnp.exp(scores[j] - peak)
        total = total + jnp.sum(e, axis=1, keepdims=True)
        values = cat[picks[j], :, D:]
        part = jnp.dot(e.astype(jnp.bfloat16), values, preferred_element_type=jnp.float32)
        acc = part if acc is None else acc + part
    lane = lax.broadcasted_iota(jnp.int32, (q.shape[0], 128), 1)
    return acc, jnp.where(lane == 0, peak, total)


def fused_kernel(
    n, reps, left_hbm, cat_hbm, slots, perm, out,
    raw, left, pout, cat, arr, slotv, slots_sm, accs, stats, acc_in, stat_in, own_acc, own_stat,
    joined, gin, pin,
    left_sem, cat_sem, slot_local, slot_send, slot_recv, f_send, f_recv,
    r_send, r_recv, s_send, s_recv, p_send, p_recv, p_local, g_send, g_recv, g_local,
):
    count = n * reps
    rows = left.shape[0]
    size = rows // CHUNKS
    each = rows // count
    s = lax.axis_index("shard")
    rep = lax.axis_index("rep")
    me = s * reps + rep
    early = is_early(s)
    px, py, pz = partner_x(s), partner_y(s), partner_z(s, n)
    pyz = partner_z(py, n)
    far = jnp.where(early, partner_x(pyz), partner_x(py))
    dests = [px, py, pyz, far]
    zs = source_z(s, n)
    xz = source_z(px, n)
    pfar = (s + 2 - 4 * (s % 2) + n) % n
    meets = [partner_y(px), py, zs, jnp.where(is_early(px), px, xz)]
    source = py * reps + rep

    def to(shard):
        return {"shard": shard, "rep": rep}

    def device(d):
        return {"shard": d // reps, "rep": d % reps}

    def remote(src, dst, send, recv, target):
        return pltpu.make_async_remote_copy(
            src_ref=src, dst_ref=dst, send_sem=send, recv_sem=recv,
            device_id=target, device_id_type=MESH,
        )

    def chunk(c):
        return pl.ds(c * size, size)

    left_copy = pltpu.make_async_copy(left_hbm, raw, left_sem)
    left_copy.start()
    def unit(u):
        return pl.ds(u * (rows // UNITS), rows // UNITS)

    cat_copy = pltpu.make_async_copy(cat_hbm, cat, cat_sem)
    cat_copy.start()
    own_slots = pltpu.make_async_copy(slots, slots_sm.at[0], slot_local.at[0])
    own_slots.start()

    barrier = pltpu.get_barrier_semaphore()

    @pl.loop(1, count)
    def _(t):
        pl.semaphore_signal(
            barrier, inc=1, device_id=device((me + t) % count), device_id_type=MESH
        )

    bf16, f32, i32 = jnp.bfloat16, jnp.float32, jnp.int32
    iota = lax.broadcasted_iota
    target = perm[...]
    device_row = target >> (rows.bit_length() - 1)
    row = target & (rows - 1)
    shard_row = device_row >> (reps.bit_length() - 1)
    side = (shard_row + (shard_row >> 1) + (shard_row >> 2)) & 1
    key = (device_row & (reps - 1)) * n + side * (n // 2) + (shard_row >> 1)
    hit = iota(i32, (count, rows), 0) == key
    hit16 = jnp.where(hit, 1.0, 0.0).astype(bf16)
    before = iota(i32, (rows, rows), 0) < iota(i32, (rows, rows), 1)
    before16 = jnp.where(before, 1.0, 0.0).astype(bf16)
    ranks = jnp.dot(hit16, before16, preferred_element_type=f32)
    rank = jnp.sum(jnp.where(hit, ranks, 0.0), axis=0, keepdims=True)
    place = key.astype(f32) * each + rank

    left_copy.wait()
    for c in range(CHUNKS):
        index = (iota(i32, (size, rows), 0) + c * size).astype(f32)
        order = jnp.where(index == place, 1.0, 0.0).astype(bf16)
        left[chunk(c)] = jnp.dot(order, raw[...], preferred_element_type=f32).astype(bf16)

    pl.semaphore_wait(barrier, count - 1)

    slot_copies = [
        remote(slots, slotv.at[a], slot_send.at[a], slot_recv.at[a], to(dests[a]))
        for a in range(ARRIVALS)
    ]
    for copy in slot_copies:
        copy.start()

    def hop(src, a, c, target):
        return remote(src, arr.at[a, chunk(c)], f_send.at[a, c], f_recv.at[a, c], to(target))

    def hop_x(c):
        return hop(left.at[chunk(c)], 0, c, px)

    def hop_y(c):
        return hop(left.at[chunk(c)], 1, c, py)

    def hop_z(c):
        return hop(arr.at[1, chunk(c)], 2, c, pz)

    def hop_far(c, a, target):
        return hop(arr.at[a, chunk(c)], 3, c, target)

    for c in range(CHUNKS):
        hop_y(c).start()
        hop_x(c).start()

    def key_of(d):
        shard = d // reps
        return (d % reps) * n + parity(shard) * (n // 2) + shard // 2

    shift = (me * each) % 128
    lanes = (iota(i32, (128, rows), 0) - shift).astype(f32)
    within = jnp.where(lanes == rank, 1.0, 0.0).astype(bf16)
    high = jnp.where(hit, (row >> 4).astype(f32), 0.0).astype(bf16)
    low = jnp.where(hit, (row & 15).astype(f32), 0.0).astype(bf16)
    rows_out = 16.0 * lax.dot_general(
        high, within, NT, preferred_element_type=f32
    ) + lax.dot_general(low, within, NT, preferred_element_type=f32)
    for g in range(count // 8):
        pout[g] = rows_out[8 * g : 8 * g + 8]
    pos_local = pltpu.make_async_copy(pout.at[key_of(me) // 8], pin.at[me], p_local)
    pos_local.start()

    @pl.loop(1, count)
    def _(t):
        d = (me + t) % count
        remote(pout.at[key_of(d) // 8], pin.at[me], p_send, p_recv, device(d)).start()

    def back(a, u):
        return (
            remote(accs.at[a, unit(u)], acc_in.at[a, unit(u)], r_send.at[a, u],
                   r_recv.at[a, u], to(meets[a])),
            remote(stats.at[a, u], stat_in.at[a, u], s_send.at[a, u],
                   s_recv.at[a, u], to(meets[a])),
        )

    def send_off(a, u, acc, stat):
        accs[a, unit(u)] = acc.astype(jnp.bfloat16)
        stats[a, u] = stat.T[:8, :]

    cat_copy.wait()
    own_slots.wait()
    for u in range(UNITS):
        send_off(1, u, *attend(left[unit(u)], cat, lambda j: slots_sm[0, 0, j]))

    for a in range(ARRIVALS):
        slot_copies[a].wait_recv()
        local = pltpu.make_async_copy(slotv.at[a], slots_sm.at[1 + a], slot_local.at[1 + a])
        local.start()
        local.wait()

    def serve(a, u):
        acc, stat = attend(arr[a, unit(u)], cat, lambda j: slots_sm[1 + a, 1 + a, j])
        if a == 1:
            own_acc[unit(u)] = acc
            own_stat[unit(u)] = stat
        else:
            send_off(a, u, acc, stat)

    def give(a, u):
        for copy in back(a, u):
            copy.start()

    def by_x(c):
        return c % 2 == 0

    def take_y(c):
        hop_y(c).wait_recv()
        hop_z(c).start()
        if by_x(c):

            @pl.when(early)
            def _():
                hop_far(c, 1, px).start()

    def take_x(c):
        hop_x(c).wait_recv()
        if not by_x(c):
            hop_far(c, 0, pfar).start()

    def take_z(c):
        hop_z(c).wait_recv()
        if by_x(c):

            @pl.when(jnp.logical_not(early))
            def _():
                hop_far(c, 2, px).start()

    take_y(0)
    take_x(0)
    take_y(1)
    take_x(1)
    take_z(0)
    serve(1, 0)
    take_y(2)
    take_z(1)
    take_x(2)
    serve(0, 0)
    take_y(3)
    take_z(2)
    take_x(3)
    serve(2, 0)
    give(2, 0)
    take_z(3)
    give(1, 0)
    give(0, 0)
    serve(1, 1)
    serve(0, 1)
    serve(2, 1)
    give(2, 1)
    per_unit = CHUNKS // UNITS
    for u in range(UNITS):
        for c in range(u * per_unit, (u + 1) * per_unit):
            hop_far(c, 1, px).wait_recv()
        serve(3, u)
        give(3, u)
        if u == 0:
            give(1, 1)
            give(0, 1)

    def lot(q):
        return pl.ds(pl.multiple_of(q * each, each), each)

    row_local = pltpu.make_async_copy(joined.at[lot(key_of(me))], gin.at[lot(source)], g_local)

    for c in range(CHUNKS):
        u = c // per_unit
        part = pl.ds(c % per_unit * size, size)
        if c % per_unit == 0:
            for a in range(ARRIVALS):
                for copy in back(a, u):
                    copy.wait_recv()
        columns = [own_stat[chunk(c)]]
        for a in range(ARRIVALS):
            columns.append(jnp.concatenate([stat_in[a, u, :, part]] * 16, axis=0).T)
        peak = columns[0][:, 0:1]
        for column in columns[1:]:
            peak = jnp.maximum(peak, column[:, 0:1])
        factor = jnp.exp(columns[0][:, 0:1] - peak)
        numer = factor * own_acc[chunk(c)]
        denom = factor * columns[0][:, 1:2]
        for a in range(ARRIVALS):
            factor = jnp.exp(columns[1 + a][:, 0:1] - peak)
            numer = numer + factor * acc_in[a, chunk(c)].astype(jnp.float32)
            denom = denom + factor * columns[1 + a][:, 1:2]
        joined[chunk(c)] = (numer / denom).astype(jnp.bfloat16)

        half = n // 2
        here = (rep - c // 2) * (rep - c // 2) + (parity(s) - c % 2) * (parity(s) - c % 2) == 0

        def row_copy(t):
            v = (s // 2 + t) % half
            return remote(
                joined.at[lot(c * half + v)], gin.at[lot(source)], g_send, g_recv,
                {"shard": of_parity(v, c % 2), "rep": c // 2},
            )

        @pl.when(jnp.logical_not(here))
        def _():
            row_copy(0).start()

        @pl.when(here)
        def _():
            row_local.start()

        @pl.loop(1, half)
        def _(t):
            row_copy(t).start()

    for u in range(UNITS):
        for a in range(ARRIVALS):
            for copy in back(a, u):
                copy.wait_send()
    for c in range(CHUNKS):
        hop_x(c).wait_send()
        hop_y(c).wait_send()
        hop_z(c).wait_send()
        hop_far(c, 1, px).wait_send()
    for copy in slot_copies:
        copy.wait_send()
    other = device((me + 1) % count)
    tiles = pin.at[pl.ds(0, count - 1)]
    pos = remote(tiles, tiles, p_send, p_recv, other)
    pos.wait_send()
    pos.wait_recv()
    pos_local.wait()
    per = 128 // each
    groups = rows // 128
    mine = iota(i32, (8, 128), 0) == key_of(me) % 8
    landing_row = iota(i32, (rows, 128), 0).astype(f32)
    spread = []
    for g in range(groups):
        tile = pin[g * per]
        for b in range(1, per):
            tile = tile + pin[g * per + b]
        landing = jnp.sum(jnp.where(mine, tile, 0.0), axis=0, keepdims=True)
        spread.append(jnp.where(landing_row == landing, 1.0, 0.0))
    spread = jnp.concatenate(spread, axis=1).astype(bf16)

    most = pl.ds(0, (count - 1) * each)
    sent = remote(joined.at[most], gin.at[most], g_send, g_recv, other)
    sent.wait_send()
    sent.wait_recv()
    row_local.wait()
    out[...] = jnp.dot(spread, gin[...], preferred_element_type=jnp.float32).astype(jnp.bfloat16)


def fused_body(left, catalog, probes, perm):
    n = lax.axis_size("shard")
    reps = lax.axis_size("rep")
    s = lax.axis_index("shard")
    rows = left.shape[0]
    count = n * reps

    py = partner_y(s)
    pyz = partner_z(py, n)
    far = jnp.where(is_early(s), partner_x(pyz), partner_x(py))
    owners = jnp.stack([s, partner_x(s), py, pyz, far])
    listed = probes[0]
    hit = (listed[None, :] >= 0) & (listed[None, :] // CB_DEV == owners[:, None])
    places = jnp.cumsum(hit.astype(jnp.int32), axis=1) - 1
    chosen = hit[:, None, :] & (places[:, None, :] == jnp.arange(CAP)[None, :, None])
    slots = jnp.max(jnp.where(chosen, listed[None, None, :] % CB_DEV, -1), axis=2)
    slots = jnp.pad(slots.astype(jnp.int32), ((0, 3), (0, 128 - CAP)))

    bf16, f32, i32 = jnp.bfloat16, jnp.float32, jnp.int32
    size = rows // CHUNKS
    dma = pltpu.SemaphoreType.DMA
    vmem = pl.BlockSpec(memory_space=pltpu.VMEM)
    return pl.pallas_call(
        functools.partial(fused_kernel, n, reps),
        out_shape=jax.ShapeDtypeStruct((rows, A), bf16),
        in_specs=[pl.BlockSpec(memory_space=pl.ANY)] * 2 + [vmem, vmem],
        out_specs=vmem,
        scratch_shapes=[
            pltpu.VMEM((rows, D), bf16),
            pltpu.VMEM((rows, D), bf16),
            pltpu.VMEM((count // 8, 8, 128), f32),
            pltpu.VMEM((CB_DEV, BLK, D + A), bf16),
            pltpu.VMEM((ARRIVALS, rows, D), bf16),
            pltpu.VMEM((ARRIVALS, 8, 128), i32),
            pltpu.SMEM((ARRIVALS + 1, 8, 128), i32),
            pltpu.VMEM((ARRIVALS, rows, A), bf16),
            pltpu.VMEM((ARRIVALS, UNITS, 8, rows // UNITS), f32),
            pltpu.VMEM((ARRIVALS, rows, A), bf16),
            pltpu.VMEM((ARRIVALS, UNITS, 8, rows // UNITS), f32),
            pltpu.VMEM((rows, A), f32),
            pltpu.VMEM((rows, 128), f32),
            pltpu.VMEM((rows, A), bf16),
            pltpu.VMEM((rows, A), bf16),
            pltpu.VMEM((count, 8, 128), f32),
            dma, dma, dma((ARRIVALS + 1,)), dma((ARRIVALS,)), dma((ARRIVALS,)),
            dma((ARRIVALS, CHUNKS)), dma((ARRIVALS, CHUNKS)),
            dma((ARRIVALS, UNITS)), dma((ARRIVALS, UNITS)),
            dma((ARRIVALS, UNITS)), dma((ARRIVALS, UNITS)),
            dma, dma, dma, dma, dma, dma,
        ],
        compiler_params=pltpu.CompilerParams(
            collective_id=0, has_side_effects=True, vmem_limit_bytes=60 * 1024 * 1024
        ),
        cost_estimate=pl.CostEstimate(
            flops=10 * rows * CAP * BLK * (D + A),
            bytes_accessed=catalog.size * 2 + rows * (D + A) * 2,
            transcendentals=5 * rows * CAP * BLK,
        ),
    )(left, catalog.reshape(CB_DEV, BLK, D + A), slots, perm.reshape(1, rows))


def body(left, catalog, probes, perm):
    n = lax.axis_size("shard")
    reps = lax.axis_size("rep")
    rows = left.shape[0]
    each = rows // (n * reps)
    if each == 16 and rows & (rows - 1) == 0 and 2 * reps == CHUNKS and n % 4 == 0 and n >= 16:
        return fused_body(left, catalog, probes, perm)
    return plain_body(left, catalog, probes, perm)


def solution(mesh):
    placed = (
        P(("shard", "rep"), None),
        P("shard", None),
        P(("shard", "rep"), None),
        P(("shard", "rep")),
    )
    return jax.shard_map(
        body, mesh=mesh, in_specs=placed, out_specs=P(("shard", "rep"), None), check_vma=False
    )
```

```python
import functools
import math

import jax
import jax.numpy as jnp
from jax import lax
from jax.experimental import pallas as pl
from jax.experimental.pallas import tpu as pltpu
from jax.sharding import PartitionSpec as P

D = 1024
A = 768
BLK = 256
CB_DEV = 8
REACH = 2
CAP = 5
SCALE = 2.5 / math.sqrt(D)
NT = (((1,), (1,)), ((), ()))


def shifted(block, axis, distance):
    devices = range(lax.axis_size(axis))
    route = [((i - distance) % len(devices), i) for i in devices]
    return lax.ppermute(block, axis, route)


def slots_for(listed, owner):
    hit = (listed >= 0) & (listed // CB_DEV == owner)
    places = jnp.cumsum(hit.astype(jnp.int32)) - 1
    chosen = hit[None, :] & (places[None, :] == jnp.arange(CAP)[:, None])
    return jnp.max(jnp.where(chosen, listed[None, :] % CB_DEV, -1), axis=1)


def group_kernel(slots_ref, q_ref, *refs):
    blocks, (acc_ref, stat_ref) = refs[:CAP], refs[CAP:]
    q = q_ref[...]
    scores = []
    for j in range(CAP):
        s = lax.dot_general(q, blocks[j][:, :D], NT, preferred_element_type=jnp.float32) * SCALE
        scores.append(jnp.where(slots_ref[j] >= 0, s, -jnp.inf))
    peak = scores[0]
    for s in scores[1:]:
        peak = jnp.maximum(peak, s)
    peak = jnp.max(peak, axis=1, keepdims=True)
    total = jnp.zeros_like(peak)
    acc = None
    for j in range(CAP):
        e = jnp.exp(scores[j] - peak)
        total = total + jnp.sum(e, axis=1, keepdims=True)
        part = jnp.dot(e.astype(jnp.bfloat16), blocks[j][:, D:], preferred_element_type=jnp.float32)
        acc = part if acc is None else acc + part
    acc_ref[...] = acc.astype(acc_ref.dtype)
    lane = lax.broadcasted_iota(jnp.int32, (q.shape[0], 128), 1)
    stat = jnp.where(lane == 0, peak, total)
    stat_ref[...] = stat.T[:8, :]


def group_partial(q, catalog, slots, dtype):
    rows = q.shape[0]
    chunk = 256
    return pl.pallas_call(
        group_kernel,
        grid_spec=pltpu.PrefetchScalarGridSpec(
            num_scalar_prefetch=1,
            grid=(rows // chunk,),
            in_specs=[pl.BlockSpec((chunk, D), lambda i, s: (i, 0))]
            + [
                pl.BlockSpec((BLK, D + A), lambda i, s, j=j: (jnp.maximum(s[j], 0), 0))
                for j in range(CAP)
            ],
            out_specs=[
                pl.BlockSpec((chunk, A), lambda i, s: (i, 0)),
                pl.BlockSpec((8, chunk), lambda i, s: (0, i)),
            ],
        ),
        out_shape=[
            jax.ShapeDtypeStruct((rows, A), dtype),
            jax.ShapeDtypeStruct((8, rows), jnp.float32),
        ],
        compiler_params=pltpu.CompilerParams(vmem_limit_bytes=40 * 1024 * 1024),
        cost_estimate=pl.CostEstimate(
            flops=2 * rows * CAP * BLK * (D + A),
            bytes_accessed=CAP * BLK * (D + A) * 2 + rows * (D + 2 * A) * 2,
            transcendentals=rows * CAP * BLK,
        ),
    )(slots, q, *([catalog] * CAP))


def plain_body(left, catalog, probes, perm):
    shard_count = lax.axis_size("shard")
    rep_count = lax.axis_size("rep")
    own = lax.axis_index("shard")
    block_rows = left.shape[0]
    devices = shard_count * rep_count
    rows_each = block_rows // devices
    offsets = (2, -2, 1, -1)
    moved = {k: shifted(left, "shard", k) for k in offsets}
    lists = {k: shifted(probes, "shard", k) for k in offsets}

    target_device = perm // block_rows
    target_row = perm % block_rows
    index = jnp.arange(block_rows)
    earlier = (target_device[:, None] == target_device[None, :]) & (index[None, :] < index[:, None])
    place = target_device * rows_each + jnp.sum(earlier.astype(jnp.int32), axis=1)
    order = place[None, :] == index[:, None]
    positions = jnp.sum(jnp.where(order, target_row[None, :], 0), axis=1).astype(jnp.int32)
    landing = lax.all_to_all(
        positions.reshape(devices, rows_each), ("shard", "rep"), 0, 0, tiled=True
    ).reshape(-1)

    parts = [group_partial(left, catalog, slots_for(probes[0], own), jnp.float32)]
    for k in offsets:
        acc, stat = group_partial(
            moved[k], catalog, slots_for(lists[k][0], own), jnp.bfloat16
        )
        parts.append((shifted(acc, "shard", -k), shifted(stat[:2], "shard", -k)))
    peak = parts[0][1][0]
    for part in parts[1:]:
        peak = jnp.maximum(peak, part[1][0])
    numer = jnp.zeros((block_rows, A), jnp.float32)
    denom = jnp.zeros((block_rows,), jnp.float32)
    for acc, stat in parts:
        factor = jnp.exp(stat[0] - peak)
        numer = numer + factor[:, None] * acc.astype(jnp.float32)
        denom = denom + factor * stat[1]
    joined = (numer / denom[:, None]).astype(jnp.bfloat16)

    outgoing = jnp.dot(
        order.astype(jnp.bfloat16), joined, preferred_element_type=jnp.float32
    ).astype(jnp.bfloat16)
    arrived = lax.all_to_all(
        outgoing.reshape(devices, rows_each, A), ("shard", "rep"), 0, 0, tiled=True
    ).reshape(block_rows, A)
    spread = (landing[None, :] == index[:, None]).astype(jnp.bfloat16)
    return jnp.dot(spread, arrived, preferred_element_type=jnp.float32).astype(jnp.bfloat16)


MESH = pl.DeviceIdType.MESH
ARRIVALS = 4
CHUNKS = 4
UNITS = 2


def partner_x(s):
    return s + 1 - 2 * (s % 2)


def partner_y(s):
    return s + 2 - 4 * ((s // 2) % 2)


def partner_z(s, n):
    return (s + 4 - 8 * ((s // 2) % 2) + n) % n


def source_z(s, n):
    return (s - 4 + 8 * ((s // 2) % 2) + n) % n


def parity(s):
    return (s + s // 2 + s // 4) % 2


def of_parity(u, p):
    return 2 * u + (p + u + u // 2) % 2


def is_early(s):
    return (s % 4) * (3 - s % 4) == 0


def attend(q, cat, slot_of):
    slots = [slot_of(j) for j in range(CAP)]
    picks = [jnp.maximum(slot, 0) for slot in slots]
    scores = []
    for j in range(CAP):
        keys = cat[picks[j], :, :D]
        s = lax.dot_general(q, keys, NT, preferred_element_type=jnp.float32) * SCALE
        scores.append(jnp.where(slots[j] >= 0, s, -jnp.inf))
    peak = scores[0]
    for s in scores[1:]:
        peak = jnp.maximum(peak, s)
    peak = jnp.max(peak, axis=1, keepdims=True)
    total = jnp.zeros_like(peak)
    acc = None
    for j in range(CAP):
        e = jnp.exp(scores[j] - peak)
        total = total + jnp.sum(e, axis=1, keepdims=True)
        values = cat[picks[j], :, D:]
        part = jnp.dot(e.astype(jnp.bfloat16), values, preferred_element_type=jnp.float32)
        acc = part if acc is None else acc + part
    lane = lax.broadcasted_iota(jnp.int32, (q.shape[0], 128), 1)
    return acc, jnp.where(lane == 0, peak, total)


def fused_kernel(
    n, reps, left_hbm, cat_hbm, slots, perm, out,
    raw, left, pout, cat, arr, slotv, slots_sm, accs, stats, acc_in, stat_in, own_acc, own_stat,
    joined, gin, pin,
    left_sem, cat_sem, slot_local, slot_send, slot_recv, f_send, f_recv,
    r_send, r_recv, s_send, s_recv, p_send, p_recv, p_local, g_send, g_recv, g_local,
):
    count = n * reps
    rows = left.shape[0]
    size = rows // CHUNKS
    each = rows // count
    s = lax.axis_index("shard")
    rep = lax.axis_index("rep")
    me = s * reps + rep
    early = is_early(s)
    px, py, pz = partner_x(s), partner_y(s), partner_z(s, n)
    pyz = partner_z(py, n)
    far = jnp.where(early, partner_x(pyz), partner_x(py))
    dests = [px, py, pyz, far]
    zs = source_z(s, n)
    xz = source_z(px, n)
    pfar = (s + 2 - 4 * (s % 2) + n) % n
    meets = [partner_y(px), py, zs, jnp.where(is_early(px), px, xz)]
    source = py * reps + rep

    def to(shard):
        return {"shard": shard, "rep": rep}

    def device(d):
        return {"shard": d // reps, "rep": d % reps}

    def remote(src, dst, send, recv, target):
        return pltpu.make_async_remote_copy(
            src_ref=src, dst_ref=dst, send_sem=send, recv_sem=recv,
            device_id=target, device_id_type=MESH,
        )

    def chunk(c):
        return pl.ds(c * size, size)

    left_copy = pltpu.make_async_copy(left_hbm, raw, left_sem)
    left_copy.start()
    def unit(u):
        return pl.ds(u * (rows // UNITS), rows // UNITS)

    cat_copy = pltpu.make_async_copy(cat_hbm, cat, cat_sem)
    cat_copy.start()
    own_slots = pltpu.make_async_copy(slots, slots_sm.at[0], slot_local.at[0])
    own_slots.start()

    barrier = pltpu.get_barrier_semaphore()

    @pl.loop(1, count)
    def _(t):
        pl.semaphore_signal(
            barrier, inc=1, device_id=device((me + t) % count), device_id_type=MESH
        )

    bf16, f32, i32 = jnp.bfloat16, jnp.float32, jnp.int32
    iota = lax.broadcasted_iota
    target = perm[...]
    device_row = target >> (rows.bit_length() - 1)
    row = target & (rows - 1)
    shard_row = device_row >> (reps.bit_length() - 1)
    side = (shard_row + (shard_row >> 1) + (shard_row >> 2)) & 1
    key = (device_row & (reps - 1)) * n + side * (n // 2) + (shard_row >> 1)
    hit = iota(i32, (count, rows), 0) == key
    hit16 = jnp.where(hit, 1.0, 0.0).astype(bf16)
    before = iota(i32, (rows, rows), 0) < iota(i32, (rows, rows), 1)
    before16 = jnp.where(before, 1.0, 0.0).astype(bf16)
    ranks = jnp.dot(hit16, before16, preferred_element_type=f32)
    rank = jnp.sum(jnp.where(hit, ranks, 0.0), axis=0, keepdims=True)
    place = key.astype(f32) * each + rank

    left_copy.wait()
    for c in range(CHUNKS):
        index = (iota(i32, (size, rows), 0) + c * size).astype(f32)
        order = jnp.where(index == place, 1.0, 0.0).astype(bf16)
        left[chunk(c)] = jnp.dot(order, raw[...], preferred_element_type=f32).astype(bf16)

    pl.semaphore_wait(barrier, count - 1)

    slot_copies = [
        remote(slots, slotv.at[a], slot_send.at[a], slot_recv.at[a], to(dests[a]))
        for a in range(ARRIVALS)
    ]
    for copy in slot_copies:
        copy.start()

    def hop(src, a, c, target):
        return remote(src, arr.at[a, chunk(c)], f_send.at[a, c], f_recv.at[a, c], to(target))

    def hop_x(c):
        return hop(left.at[chunk(c)], 0, c, px)

    def hop_y(c):
        return hop(left.at[chunk(c)], 1, c, py)

    def hop_z(c):
        return hop(arr.at[1, chunk(c)], 2, c, pz)

    def hop_far(c, a, target):
        return hop(arr.at[a, chunk(c)], 3, c, target)

    def launch(c):
        if c > 0:
            hop_y(c - 1).wait_send()
            hop_x(c - 1).wait_send()
        hop_y(c).start()
        hop_x(c).start()

    launch(0)

    def key_of(d):
        shard = d // reps
        return (d % reps) * n + parity(shard) * (n // 2) + shard // 2

    shift = (me * each) % 128
    lanes = (iota(i32, (128, rows), 0) - shift).astype(f32)
    within = jnp.where(lanes == rank, 1.0, 0.0).astype(bf16)
    high = jnp.where(hit, (row >> 4).astype(f32), 0.0).astype(bf16)
    low = jnp.where(hit, (row & 15).astype(f32), 0.0).astype(bf16)
    rows_out = 16.0 * lax.dot_general(
        high, within, NT, preferred_element_type=f32
    ) + lax.dot_general(low, within, NT, preferred_element_type=f32)
    for g in range(count // 8):
        pout[g] = rows_out[8 * g : 8 * g + 8]
    pos_local = pltpu.make_async_copy(pout.at[key_of(me) // 8], pin.at[me], p_local)
    pos_local.start()

    @pl.loop(1, count)
    def _(t):
        d = (me + t) % count
        remote(pout.at[key_of(d) // 8], pin.at[me], p_send, p_recv, device(d)).start()

    def back(a, u):
        return (
            remote(accs.at[a, unit(u)], acc_in.at[a, unit(u)], r_send.at[a, u],
                   r_recv.at[a, u], to(meets[a])),
            remote(stats.at[a, u], stat_in.at[a, u], s_send.at[a, u],
                   s_recv.at[a, u], to(meets[a])),
        )

    def send_off(a, u, acc, stat):
        accs[a, unit(u)] = acc.astype(jnp.bfloat16)
        stats[a, u] = stat.T[:8, :]

    cat_copy.wait()
    own_slots.wait()
    for u in range(UNITS):
        send_off(1, u, *attend(left[unit(u)], cat, lambda j: slots_sm[0, 0, j]))
        if u == 0:
            launch(1)

    for a in range(ARRIVALS):
        slot_copies[a].wait_recv()
        local = pltpu.make_async_copy(slotv.at[a], slots_sm.at[1 + a], slot_local.at[1 + a])
        local.start()
        local.wait()

    def serve(a, u):
        acc, stat = attend(arr[a, unit(u)], cat, lambda j: slots_sm[1 + a, 1 + a, j])
        if a == 1:
            own_acc[unit(u)] = acc
            own_stat[unit(u)] = stat
        else:
            send_off(a, u, acc, stat)

    def give(a, u):
        for copy in back(a, u):
            copy.start()

    def by_x(c):
        return c % 2 == 0

    def take_y(c):
        hop_y(c).wait_recv()
        hop_z(c).start()
        if by_x(c):

            @pl.when(early)
            def _():
                hop_far(c, 1, px).start()

    def take_x(c):
        hop_x(c).wait_recv()
        if not by_x(c):
            hop_far(c, 0, pfar).start()

    def take_z(c):
        hop_z(c).wait_recv()
        if by_x(c):

            @pl.when(jnp.logical_not(early))
            def _():
                hop_far(c, 2, px).start()

    take_y(0)
    take_x(0)
    launch(2)
    take_z(0)
    take_y(1)
    take_x(1)
    serve(1, 0)
    launch(3)
    take_z(1)
    take_y(2)
    take_x(2)
    serve(0, 0)
    take_z(2)
    take_y(3)
    take_x(3)
    serve(2, 0)
    give(2, 0)
    take_z(3)
    give(1, 0)
    give(0, 0)
    serve(1, 1)
    serve(0, 1)
    serve(2, 1)
    give(2, 1)
    per_unit = CHUNKS // UNITS
    for u in range(UNITS):
        for c in range(u * per_unit, (u + 1) * per_unit):
            hop_far(c, 1, px).wait_recv()
        serve(3, u)
        give(3, u)
        if u == 0:
            give(1, 1)
            give(0, 1)

    def lot(q):
        return pl.ds(pl.multiple_of(q * each, each), each)

    row_local = pltpu.make_async_copy(joined.at[lot(key_of(me))], gin.at[lot(source)], g_local)

    for c in range(CHUNKS):
        u = c // per_unit
        part = pl.ds(c % per_unit * size, size)
        if c % per_unit == 0:
            for a in range(ARRIVALS):
                for copy in back(a, u):
                    copy.wait_recv()
        columns = [own_stat[chunk(c)]]
        for a in range(ARRIVALS):
            columns.append(jnp.concatenate([stat_in[a, u, :, part]] * 16, axis=0).T)
        peak = columns[0][:, 0:1]
        for column in columns[1:]:
            peak = jnp.maximum(peak, column[:, 0:1])
        factor = jnp.exp(columns[0][:, 0:1] - peak)
        numer = factor * own_acc[chunk(c)]
        denom = factor * columns[0][:, 1:2]
        for a in range(ARRIVALS):
            factor = jnp.exp(columns[1 + a][:, 0:1] - peak)
            numer = numer + factor * acc_in[a, chunk(c)].astype(jnp.float32)
            denom = denom + factor * columns[1 + a][:, 1:2]
        joined[chunk(c)] = (numer / denom).astype(jnp.bfloat16)

        half = n // 2
        here = (rep - c // 2) * (rep - c // 2) + (parity(s) - c % 2) * (parity(s) - c % 2) == 0

        def row_copy(t):
            v = (s // 2 + t) % half
            return remote(
                joined.at[lot(c * half + v)], gin.at[lot(source)], g_send, g_recv,
                {"shard": of_parity(v, c % 2), "rep": c // 2},
            )

        @pl.when(jnp.logical_not(here))
        def _():
            row_copy(0).start()

        @pl.when(here)
        def _():
            row_local.start()

        @pl.loop(1, half)
        def _(t):
            row_copy(t).start()

    for u in range(UNITS):
        for a in range(ARRIVALS):
            for copy in back(a, u):
                copy.wait_send()
    for c in range(CHUNKS):
        if c == CHUNKS - 1:
            hop_x(c).wait_send()
            hop_y(c).wait_send()
        hop_z(c).wait_send()
        hop_far(c, 1, px).wait_send()
    for copy in slot_copies:
        copy.wait_send()
    other = device((me + 1) % count)
    tiles = pin.at[pl.ds(0, count - 1)]
    pos = remote(tiles, tiles, p_send, p_recv, other)
    pos.wait_send()
    pos.wait_recv()
    pos_local.wait()
    per = 128 // each
    groups = rows // 128
    mine = iota(i32, (8, 128), 0) == key_of(me) % 8
    landing_row = iota(i32, (rows, 128), 0).astype(f32)
    spread = []
    for g in range(groups):
        tile = pin[g * per]
        for b in range(1, per):
            tile = tile + pin[g * per + b]
        landing = jnp.sum(jnp.where(mine, tile, 0.0), axis=0, keepdims=True)
        spread.append(jnp.where(landing_row == landing, 1.0, 0.0))
    spread = jnp.concatenate(spread, axis=1).astype(bf16)

    most = pl.ds(0, (count - 1) * each)
    sent = remote(joined.at[most], gin.at[most], g_send, g_recv, other)
    sent.wait_send()
    sent.wait_recv()
    row_local.wait()
    out[...] = jnp.dot(spread, gin[...], preferred_element_type=jnp.float32).astype(jnp.bfloat16)


def fused_body(left, catalog, probes, perm):
    n = lax.axis_size("shard")
    reps = lax.axis_size("rep")
    s = lax.axis_index("shard")
    rows = left.shape[0]
    count = n * reps

    py = partner_y(s)
    pyz = partner_z(py, n)
    far = jnp.where(is_early(s), partner_x(pyz), partner_x(py))
    owners = jnp.stack([s, partner_x(s), py, pyz, far])
    listed = probes[0]
    hit = (listed[None, :] >= 0) & (listed[None, :] // CB_DEV == owners[:, None])
    places = jnp.cumsum(hit.astype(jnp.int32), axis=1) - 1
    chosen = hit[:, None, :] & (places[:, None, :] == jnp.arange(CAP)[None, :, None])
    slots = jnp.max(jnp.where(chosen, listed[None, None, :] % CB_DEV, -1), axis=2)
    slots = jnp.pad(slots.astype(jnp.int32), ((0, 3), (0, 128 - CAP)))

    bf16, f32, i32 = jnp.bfloat16, jnp.float32, jnp.int32
    size = rows // CHUNKS
    dma = pltpu.SemaphoreType.DMA
    vmem = pl.BlockSpec(memory_space=pltpu.VMEM)
    return pl.pallas_call(
        functools.partial(fused_kernel, n, reps),
        out_shape=jax.ShapeDtypeStruct((rows, A), bf16),
        in_specs=[pl.BlockSpec(memory_space=pl.ANY)] * 2 + [vmem, vmem],
        out_specs=vmem,
        scratch_shapes=[
            pltpu.VMEM((rows, D), bf16),
            pltpu.VMEM((rows, D), bf16),
            pltpu.VMEM((count // 8, 8, 128), f32),
            pltpu.VMEM((CB_DEV, BLK, D + A), bf16),
            pltpu.VMEM((ARRIVALS, rows, D), bf16),
            pltpu.VMEM((ARRIVALS, 8, 128), i32),
            pltpu.SMEM((ARRIVALS + 1, 8, 128), i32),
            pltpu.VMEM((ARRIVALS, rows, A), bf16),
            pltpu.VMEM((ARRIVALS, UNITS, 8, rows // UNITS), f32),
            pltpu.VMEM((ARRIVALS, rows, A), bf16),
            pltpu.VMEM((ARRIVALS, UNITS, 8, rows // UNITS), f32),
            pltpu.VMEM((rows, A), f32),
            pltpu.VMEM((rows, 128), f32),
            pltpu.VMEM((rows, A), bf16),
            pltpu.VMEM((rows, A), bf16),
            pltpu.VMEM((count, 8, 128), f32),
            dma, dma, dma((ARRIVALS + 1,)), dma((ARRIVALS,)), dma((ARRIVALS,)),
            dma((ARRIVALS, CHUNKS)), dma((ARRIVALS, CHUNKS)),
            dma((ARRIVALS, UNITS)), dma((ARRIVALS, UNITS)),
            dma((ARRIVALS, UNITS)), dma((ARRIVALS, UNITS)),
            dma, dma, dma, dma, dma, dma,
        ],
        compiler_params=pltpu.CompilerParams(
            collective_id=0, has_side_effects=True, vmem_limit_bytes=60 * 1024 * 1024
        ),
        cost_estimate=pl.CostEstimate(
            flops=10 * rows * CAP * BLK * (D + A),
            bytes_accessed=catalog.size * 2 + rows * (D + A) * 2,
            transcendentals=5 * rows * CAP * BLK,
        ),
    )(left, catalog.reshape(CB_DEV, BLK, D + A), slots, perm.reshape(1, rows))


def body(left, catalog, probes, perm):
    n = lax.axis_size("shard")
    reps = lax.axis_size("rep")
    rows = left.shape[0]
    each = rows // (n * reps)
    if each == 16 and rows & (rows - 1) == 0 and 2 * reps == CHUNKS and n % 4 == 0 and n >= 16:
        return fused_body(left, catalog, probes, perm)
    return plain_body(left, catalog, probes, perm)


def solution(mesh):
    placed = (
        P(("shard", "rep"), None),
        P("shard", None),
        P(("shard", "rep"), None),
        P(("shard", "rep")),
    )
    return jax.shard_map(
        body, mesh=mesh, in_specs=placed, out_specs=P(("shard", "rep"), None), check_vma=False
    )
```
